32 devices in a mesh: groups: 2 (over y), dp: 4 (over x, core), tensor: 4 (over z).
Axes of the slice: x: 2, y: 2, z: 4, core: 2. Of those that a mesh axis runs over, the one named last changes fastest.
Arguments:
- hidden_first: bfloat16 [32, 16384], P('groups', 'dp'), parts along dimension 0, may hold values from -6 to 6
- hidden_second: bfloat16 [32, 16384], P('groups', 'dp'), parts along dimension 0, may hold values from -6 to 6
- norm_gain: bfloat16 [16384], P('dp'), may hold values from 0.25 to 1.75
- query_weight: bfloat16 [16384, 16384], P('dp', 'tensor'), may hold values from -0.0625 to 0.0625
- w_key: bfloat16 [16384, 1024], P('dp', 'tensor'), may hold values from -0.046875 to 0.046875
- w_value: bfloat16 [16384, 1024], P('dp', 'tensor'), may hold values from -0.046875 to 0.046875
- w_out: bfloat16 [16384, 16384], P('tensor', 'dp'), may hold values from -0.046875 to 0.046875
- a_query: bfloat16 [16384, 128], P(('dp', 'tensor')), may hold values from -0.046875 to 0.046875
- b_query: bfloat16 [128, 16384], P(None, ('tensor', 'dp')), may hold values from -0.1796875 to 0.1796875
- a_key: bfloat16 [16384, 128], P(('dp', 'tensor')), may hold values from -0.046875 to 0.046875
- b_key: bfloat16 [128, 1024], P(None, ('tensor', 'dp')), may hold values from -0.1796875 to 0.1796875
- a_value: bfloat16 [16384, 128], P(('dp', 'tensor')), may hold values from -0.046875 to 0.046875
- b_value: bfloat16 [128, 1024], P(None, ('tensor', 'dp')), may hold values from -0.1796875 to 0.1796875
- a_out: bfloat16 [16384, 128], P(('tensor', 'dp')), may hold values from -0.046875 to 0.046875
- b_out: bfloat16 [128, 16384], P(None, ('dp', 'tensor')), may hold values from -0.1796875 to 0.1796875
- cache_keys: bfloat16 [32, 8, 192, 128], P(('groups', 'dp'), None, 'tensor'), parts along dimension 0, may hold values from -6 to 6
- cache_values: bfloat16 [32, 8, 192, 128], P(('groups', 'dp'), None, 'tensor'), parts along dimension 0, may hold values from -6 to 6
- lengths: int32 [32], P(('groups', 'dp')), parts along dimension 0, may hold values from 1 to 192, as said below
Outputs:
- attn_first: bfloat16 [32, 16384], P('groups', 'dp'), parts along dimension 0
- attn_second: bfloat16 [32, 16384], P('groups', 'dp'), parts along dimension 0
The draws below stay inside these ranges and needn't reach their ends.
There are 2 independent parts, one for each index of `groups`. The reference program is written for one: setup_inputs(seed, part) draws one part's arguments, and reference() takes and returns one part's arrays. A program takes and returns all parts, laid end to end along the dimension named above; an argument that names none is the same for every part. Nothing has to cross between parts.
Inputs may be any that keep to these rules, and one draw needn't show every extreme that they name: `lengths`: cache positions below a row's length hold its earlier tokens; some row of each part uses all 192 positions.
All inputs are finite; a program needn't handle non-finite values.
Results may differ from the reference program's by a relative error of at most 0.0087.
Values may be sent and summed in bfloat16 or wider, within the bound.
No kernel may reach another device: no remote copies, remote signals or barrier semaphores. Data moves between devices by JAX's collectives and lax.ppermute only.
A program may use at most 320 MiB of HBM per device.

```python
import math
import jax
import jax.numpy as jnp
from jax import lax

D = 16384
HQ = 128
KVH = 8
HD = 128
R = 128
ROWS = 16
CACHE = 192
QC = 16384
KC = 1024


def row_lengths(key):
    key = jax.random.fold_in(key, 7)
    first_key, second_key = jax.random.split(key)
    drawn = jax.random.randint(first_key, (ROWS,), 1, CACHE + 1)
    chosen = jax.random.randint(second_key, (), 0, ROWS)
    return jnp.where(jnp.arange(ROWS) == chosen, CACHE, drawn).astype(jnp.int32)


def feature_ramp(low, high):
    place = jnp.arange(D, dtype=jnp.float32) / D
    return low * (high / low) ** place


def ramped_normal(key):
    values = jax.random.normal(key, (ROWS, D), jnp.float32) * feature_ramp(0.6, 2.4)[None, :]
    return jnp.clip(values, -6.0, 6.0)


def draw_lengths(key, part):
    return row_lengths(key)


def draw_hidden_first(key, part):
    key = jax.random.fold_in(key, 31)
    return ramped_normal(key).astype(jnp.bfloat16)


def draw_hidden_second(key, part):
    key = jax.random.fold_in(key, 37)
    return ramped_normal(key).astype(jnp.bfloat16)


def draw_query_weight(key, part):
    key = jax.random.fold_in(key, 41)
    return (jnp.clip(jax.random.normal(key, (D, QC), jnp.float32), -6.0, 6.0) / D ** 0.5).astype(jnp.bfloat16)


def draw_cache_keys(key, part):
    key = jax.random.fold_in(key, 43)
    return jnp.clip(jax.random.normal(key, (ROWS, KVH, CACHE, HD), jnp.float32), -6.0, 6.0).astype(jnp.bfloat16)


def block_levels(key, shape, cuts, least, high):
    def one(axis_at, parts):
        draws = jax.random.uniform(jax.random.fold_in(jax.random.fold_in(key, 6), axis_at), (parts,), jnp.float32, least / len(cuts), high / len(cuts))
        return jnp.repeat(jnp.exp(draws), shape[axis_at] // parts).reshape((-1,) + (1,) * (len(shape) - axis_at - 1))

    factor_of = one(*cuts[0])
    for cut in cuts[1:]:
        factor_of = factor_of * one(*cut)
    return factor_of


def normal_values(stream_key, shape, deviation, limit, cuts=(), held_as=jnp.bfloat16):
    values = deviation * jax.random.normal(stream_key, shape, jnp.float32)
    if cuts:
        values = values * block_levels(stream_key, shape, cuts, -0.22, 0.18)
    return jnp.clip(values, -limit, limit).astype(held_as)


def setup_inputs(seed: int = 0, part: int = 0) -> dict:
    seeds = jax.random.split(jax.random.key(seed), 19)
    part_splits = jax.random.split(jax.random.fold_in(seeds[18], part), 19)
    return {
        "hidden_first": draw_hidden_first(jax.random.fold_in(jax.random.fold_in(seeds[18], part), 71), part),
        "hidden_second": draw_hidden_second(jax.random.fold_in(jax.random.fold_in(seeds[18], part), 71), part),
        "norm_gain": jnp.clip(1.0 + 0.15 * jax.random.normal(seeds[2], (D,), jnp.float32), 0.25, 1.75).astype(jnp.bfloat16),
        "query_weight": draw_query_weight(jax.random.fold_in(seeds[18], 71), part),
        "w_key": normal_values(seeds[4], (D, KC), D ** -0.5, 0.046875, ((0, 4), (1, 4))),
        "w_value": normal_values(seeds[5], (D, KC), D ** -0.5, 0.046875, ((0, 4), (1, 4))),
        "w_out": normal_values(seeds[6], (QC, D), QC ** -0.5, 0.046875, ((0, 4), (1, 4))),
        "a_query": normal_values(seeds[7], (D, R), D ** -0.5, 0.046875, ((0, 16),)),
        "b_query": normal_values(seeds[8], (R, QC), 0.03, 0.1796875, ((1, 16),)),
        "a_key": normal_values(seeds[9], (D, R), D ** -0.5, 0.046875, ((0, 16),)),
        "b_key": normal_values(seeds[10], (R, KC), 0.03, 0.1796875, ((1, 16),)),
        "a_value": normal_values(seeds[11], (D, R), D ** -0.5, 0.046875, ((0, 16),)),
        "b_value": normal_values(seeds[12], (R, KC), 0.03, 0.1796875, ((1, 16),)),
        "a_out": normal_values(seeds[13], (QC, R), QC ** -0.5, 0.046875, ((0, 16),)),
        "b_out": normal_values(seeds[14], (R, D), 0.03, 0.1796875, ((1, 16),)),
        "cache_keys": draw_cache_keys(jax.random.fold_in(jax.random.fold_in(seeds[18], part), 71), part),
        "cache_values": normal_values(part_splits[16], (ROWS, KVH, CACHE, HD), 1.0, 6.0, ((0, 4), (2, 4))),
        "lengths": draw_lengths(jax.random.fold_in(jax.random.fold_in(seeds[18], part), 71), part),
    }


ADAPTER_SCALE = 2.0
ROPE_BASE = 500000.0
EPS = 1e-05
MASKED_FILLER = -1e+30

def merge_weight(frozen_weight, factor_in, factor_out):
    adapter_update = jnp.dot(factor_in, factor_out, preferred_element_type=jnp.float32)
    return (frozen_weight.astype(jnp.float32) + ADAPTER_SCALE * adapter_update).astype(jnp.bfloat16)

def rotary(vectors, positions_now):
    half_dim = vectors.shape[-1] // 2
    frequency = ROPE_BASE ** (-jnp.arange(half_dim, dtype=jnp.float32) / half_dim)
    angles = positions_now.astype(jnp.float32)[:, None] * frequency[None, :]
    cosine = jnp.cos(angles)[:, None, :]
    sine_part = jnp.sin(angles)[:, None, :]
    lower = vectors[..., :half_dim]
    upper = vectors[..., half_dim:]
    return jnp.concatenate([lower * cosine - upper * sine_part, upper * cosine + lower * sine_part], axis=-1)

def normalize(hidden, norm_gain):
    values_f = hidden.astype(jnp.float32)
    squares = lax.optimization_barrier(jnp.sum(values_f * values_f, axis=1))
    return (values_f * lax.rsqrt(squares / D + EPS)[:, None] * norm_gain.astype(jnp.float32)).astype(jnp.bfloat16)

def project(normed, frozen_weight, factor_in, factor_out):
    columns = frozen_weight.shape[1]
    width = math.gcd(columns, 1024)
    blocks = columns // width
    frozen_blocks = frozen_weight.reshape(frozen_weight.shape[0], blocks, width).transpose(1, 0, 2)
    out_blocks = factor_out.reshape(factor_out.shape[0], blocks, width).transpose(1, 0, 2)

    def one_block(pair):
        weight = merge_weight(pair[0], factor_in, pair[1])
        return jnp.dot(normed, weight, preferred_element_type=jnp.float32)
    result = lax.map(one_block, (frozen_blocks, out_blocks))
    return result.transpose(1, 0, 2).reshape(normed.shape[0], columns)

def reference(hidden_first, hidden_second, norm_gain, query_weight, w_key, w_value, w_out, a_query, b_query, a_key, b_key, a_value, b_value, a_out, b_out, cache_keys, cache_values, lengths):
    row_count = hidden_first.shape[0]
    normed = jnp.concatenate([normalize(hidden_first, norm_gain), normalize(hidden_second, norm_gain)], axis=0)
    queries = project(normed, query_weight, a_query, b_query).astype(jnp.bfloat16)
    keys_all = project(normed, w_key, a_key, b_key).astype(jnp.bfloat16)
    values_all = project(normed, w_value, a_value, b_value).astype(jnp.bfloat16)
    score_scale = 1.0 / math.sqrt(HD)
    cache_kf = cache_keys.astype(jnp.float32)
    cache_vf = cache_values.astype(jnp.float32)
    cache_valid = jnp.arange(CACHE, dtype=jnp.int32)[None, :] < lengths[:, None]
    fresh_keys = []
    fresh_values = []
    heads_out = []
    for step_index in range(2):
        positions_now = lengths + step_index
        lower_row = step_index * row_count
        query_now = queries[lower_row:lower_row + row_count].reshape(row_count, HQ, HD).astype(jnp.float32)
        query_now = lax.optimization_barrier(rotary(query_now, positions_now).astype(jnp.bfloat16))
        query_now = query_now.astype(jnp.float32).reshape(row_count, KVH, HQ // KVH, HD)
        key_now = keys_all[lower_row:lower_row + row_count].reshape(row_count, KVH, HD).astype(jnp.float32)
        fresh_keys.append(rotary(key_now, positions_now).astype(jnp.bfloat16))
        fresh_values.append(values_all[lower_row:lower_row + row_count].reshape(row_count, KVH, HD))
        cache_scores = jnp.einsum('rkgd,rksd->rkgs', query_now, cache_kf) * score_scale
        cache_scores = jnp.where(cache_valid[:, None, None, :], cache_scores, MASKED_FILLER)
        new_keys = jnp.stack(fresh_keys, axis=2).astype(jnp.float32)
        new_values = jnp.stack(fresh_values, axis=2).astype(jnp.float32)
        new_scores = jnp.einsum('rkgd,rknd->rkgn', query_now, new_keys) * score_scale
        highest = jnp.maximum(lax.optimization_barrier(jnp.max(cache_scores, axis=-1)), lax.optimization_barrier(jnp.max(new_scores, axis=-1)))
        cache_weights = jnp.where(cache_valid[:, None, None, :], jnp.exp(cache_scores - highest[..., None]), 0.0)
        new_weights = jnp.exp(new_scores - highest[..., None])
        totals = lax.optimization_barrier(jnp.sum(cache_weights, axis=-1)) + lax.optimization_barrier(jnp.sum(new_weights, axis=-1))
        weighted = jnp.einsum('rkgs,rksd->rkgd', cache_weights, cache_vf) + jnp.einsum('rkgn,rknd->rkgd', new_weights, new_values)
        heads_out.append((weighted / totals[..., None]).reshape(row_count, QC).astype(jnp.bfloat16))
    output = project(jnp.concatenate(heads_out, axis=0), w_out, a_out, b_out).astype(jnp.bfloat16)
    return (output[:row_count], output[row_count:])
```

```python
import functools
import math

import jax
import jax.numpy as jnp
import numpy as np
from jax import lax
from jax.experimental import pallas as pl
from jax.experimental.pallas import tpu as pltpu
from jax.sharding import PartitionSpec as P

D = 16384


ADAPTER_SCALE = 2.0
ROPE_BASE = 500000.0
EPS = 1e-05
MASKED_FILLER = -1e30
BF16 = jnp.bfloat16
F32 = jnp.float32


def joined_2(part, axis, combine):
    gathered = jax.tree.map(lambda a: lax.all_gather(a, axis), part)

    def take(source):
        return jax.tree.map(lambda a: lax.dynamic_index_in_dim(a, source, 0, False), gathered)

    return lax.fori_loop(
        1, lax.axis_size(axis), lambda source, state: combine(state, take(source)), take(0)
    )


def merge_weight(frozen_weight, factor_in, factor_out):
    adapter_update = jnp.dot(factor_in, factor_out, preferred_element_type=jnp.float32)
    return (frozen_weight.astype(jnp.float32) + ADAPTER_SCALE * adapter_update).astype(jnp.bfloat16)


def rotary(vectors, positions_now):
    half_dim = vectors.shape[-1] // 2
    frequency = ROPE_BASE ** (-jnp.arange(half_dim, dtype=jnp.float32) / half_dim)
    angles = positions_now.astype(jnp.float32)[:, None] * frequency[None, :]
    cosine = jnp.cos(angles)[:, None, :]
    sine_part = jnp.sin(angles)[:, None, :]
    lower = vectors[..., :half_dim]
    upper = vectors[..., half_dim:]
    return jnp.concatenate(
        [lower * cosine - upper * sine_part, upper * cosine + lower * sine_part], axis=-1
    )


def combine_partial(earlier, later):
    highest = jnp.maximum(earlier[0], later[0])
    weight_a = jnp.exp(earlier[0] - highest)
    weight_b = jnp.exp(later[0] - highest)
    return (
        highest,
        earlier[1] * weight_a + later[1] * weight_b,
        earlier[2] * weight_a[..., None] + later[2] * weight_b[..., None],
    )


def on_device(
    hidden_first,
    hidden_second,
    norm_gain,
    query_weight,
    w_key,
    w_value,
    w_out,
    a_query,
    b_query,
    a_key,
    b_key,
    a_value,
    b_value,
    a_out,
    b_out,
    cache_keys,
    cache_values,
    lengths,
):
    tensor_parts = (
        lax.all_gather(a_query, "tensor", axis=0, tiled=True),
        lax.all_gather(a_key, "tensor", axis=0, tiled=True),
        lax.all_gather(a_value, "tensor", axis=0, tiled=True),
        lax.all_gather(b_out, "tensor", axis=1, tiled=True),
    )
    data_parts = (
        lax.all_gather(b_query, "dp", axis=1, tiled=True),
        lax.all_gather(b_key, "dp", axis=1, tiled=True),
        lax.all_gather(b_value, "dp", axis=1, tiled=True),
        lax.all_gather(a_out, "dp", axis=0, tiled=True),
    )
    merged_qkv = jnp.concatenate(
        [
            merge_weight(query_weight, tensor_parts[0], data_parts[0]),
            merge_weight(w_key, tensor_parts[1], data_parts[1]),
            merge_weight(w_value, tensor_parts[2], data_parts[2]),
        ],
        axis=1,
    )
    merged_output = merge_weight(w_out, data_parts[3], tensor_parts[3])
    n_tensor = lax.axis_size("tensor")
    tensor_index = lax.axis_index("tensor")
    rows_dev, key_value_heads, cache_span, head_dim = cache_keys.shape
    query_cols = query_weight.shape[1]
    key_cols = w_key.shape[1]
    joint_cols = query_cols + 2 * key_cols
    heads_here = query_cols // head_dim
    all_heads = heads_here * n_tensor
    group_size = all_heads // key_value_heads
    score_scale = 1.0 / math.sqrt(head_dim)
    cache_positions = tensor_index * cache_span + jnp.arange(cache_span, dtype=jnp.int32)
    cache_valid = cache_positions[None, :] < lengths[:, None]
    first_owner = tensor_index == 0
    fresh_keys = []
    fresh_values = []
    results = []
    for step_index, hidden in enumerate((hidden_first, hidden_second)):
        values_f = hidden.astype(jnp.float32)
        squares = lax.psum(jnp.sum(values_f * values_f, axis=1), "dp")
        normed = (
            values_f * lax.rsqrt(squares / D + EPS)[:, None] * norm_gain.astype(jnp.float32)
        ).astype(jnp.bfloat16)
        projected = lax.psum_scatter(
            jnp.dot(normed, merged_qkv, preferred_element_type=jnp.float32),
            "dp",
            scatter_dimension=0,
            tiled=True,
        ).astype(jnp.bfloat16)
        joined = lax.all_gather(projected, "tensor", axis=1, tiled=True).reshape(
            rows_dev, n_tensor, joint_cols
        )
        queries = joined[:, :, :query_cols].reshape(rows_dev, all_heads, head_dim)
        key_now = joined[:, :, query_cols : query_cols + key_cols].reshape(
            rows_dev, key_value_heads, head_dim
        )
        value_now = joined[:, :, query_cols + key_cols :].reshape(
            rows_dev, key_value_heads, head_dim
        )
        positions_now = lengths + step_index
        queries = rotary(queries.astype(jnp.float32), positions_now).astype(jnp.bfloat16)
        queries = queries.reshape(rows_dev, key_value_heads, group_size, head_dim)
        fresh_keys.append(rotary(key_now.astype(jnp.float32), positions_now).astype(jnp.bfloat16))
        fresh_values.append(value_now)
        cache_scores = (
            jnp.einsum("rkgd,rksd->rkgs", queries, cache_keys, preferred_element_type=jnp.float32)
            * score_scale
        )
        cache_scores = jnp.where(cache_valid[:, None, None, :], cache_scores, MASKED_FILLER)
        new_scores = (
            jnp.einsum(
                "rkgd,rknd->rkgn",
                queries,
                jnp.stack(fresh_keys, axis=2),
                preferred_element_type=jnp.float32,
            )
            * score_scale
        )
        new_scores = jnp.where(first_owner, new_scores, MASKED_FILLER)
        highest = jnp.maximum(jnp.max(cache_scores, axis=-1), jnp.max(new_scores, axis=-1))
        cache_weights = jnp.where(
            cache_valid[:, None, None, :], jnp.exp(cache_scores - highest[..., None]), 0.0
        )
        new_weights = jnp.where(first_owner, jnp.exp(new_scores - highest[..., None]), 0.0)
        totals = jnp.sum(cache_weights, axis=-1) + jnp.sum(new_weights, axis=-1)
        weighted = jnp.einsum(
            "rkgs,rksd->rkgd", cache_weights, cache_values, preferred_element_type=jnp.float32
        )
        weighted = weighted + jnp.einsum(
            "rkgn,rknd->rkgd",
            new_weights,
            jnp.stack(fresh_values, axis=2),
            preferred_element_type=jnp.float32,
        )
        highest = highest.reshape(rows_dev, all_heads)
        totals = totals.reshape(rows_dev, all_heads)
        weighted = weighted.reshape(rows_dev, all_heads, head_dim)
        high_all, total_all, weighted_all = joined_2(
            (highest, totals, weighted), "tensor", combine_partial
        )
        normalized = weighted_all / total_all[..., None]
        own_heads = lax.dynamic_slice_in_dim(normalized, tensor_index * heads_here, heads_here, 1)
        heads = own_heads.reshape(rows_dev, query_cols).astype(jnp.bfloat16)
        out_terms = jnp.dot(
            lax.all_gather(heads, "dp", axis=0, tiled=True),
            merged_output,
            preferred_element_type=jnp.float32,
        )
        attn_out = lax.psum(out_terms, "tensor").astype(jnp.bfloat16)
        results.append(attn_out)
    return (results[0], results[1])

def swapped(array, axis, mask):
    size = lax.axis_size(axis)
    return lax.ppermute(array, axis, [(k, k ^ mask) for k in range(size)])


def vmem_spec():
    return pl.BlockSpec(memory_space=pltpu.VMEM)


def hbm_spec():
    return pl.BlockSpec(memory_space=pltpu.HBM)


def in_hbm(*arrays):
    return [pltpu.with_memory_space_constraint(array, pltpu.HBM) for array in arrays]


def cost(moved):
    return pl.CostEstimate(flops=0, bytes_accessed=int(moved), transcendentals=0)


def kernel_call(body, outs, in_specs, scratch=(), mib=24, out_specs=None, moved=0):
    return pl.pallas_call(
        body,
        out_shape=outs,
        in_specs=in_specs,
        out_specs=out_specs or tuple(vmem_spec() for _ in outs),
        scratch_shapes=list(scratch),
        cost_estimate=cost(moved),
        compiler_params=pltpu.CompilerParams(vmem_limit_bytes=mib << 20),
    )


def aligned(start, size, unit):
    return pl.ds(pl.multiple_of(start, unit), size)


def split_sum(total, width):
    high = total.astype(BF16).astype(F32)
    rest = total - high
    middle = rest.astype(BF16).astype(F32)
    low = rest - middle
    lane = lax.broadcasted_iota(jnp.int32, (total.shape[0], width), 1)
    return jnp.where(
        lane == 0, high, jnp.where(lane == 1, middle, jnp.where(lane == 2, low, 0.0))
    )


def prepare_body(
    rows_dev,
    first_ref,
    second_ref,
    gain_ref,
    a_query_ref,
    a_key_ref,
    a_value_ref,
    keys_ref,
    values_ref,
    b_query_ref,
    b_key_ref,
    b_value_ref,
    a_out_ref,
    scaled_ref,
    squares_ref,
    low_ref,
    near,
    far_1,
    far_2,
    far_3,
    factors_ref,
    hidden,
    gain_held,
    a_held,
    sems,
):
    tensor_index = lax.axis_index("tensor")
    heads_here = keys_ref.shape[1] // lax.axis_size("tensor")
    rank = a_query_ref.shape[1]
    wide = b_query_ref.shape[1]
    narrow = b_key_ref.shape[0]

    def begun(group, pairs):
        copies = [pltpu.make_async_copy(*pair, sems.at[group]) for pair in pairs]
        for copy in copies:
            copy.start()
        return copies

    inputs = begun(
        0, [(first_ref, hidden.at[0]), (second_ref, hidden.at[1]), (gain_ref, gain_held)]
    )
    inputs += begun(
        1,
        [(ref, a_held.at[place]) for place, ref in enumerate((a_query_ref, a_key_ref, a_value_ref))],
    )
    moves = []
    for mask, far in enumerate((near, far_1, far_2, far_3)):
        head = jnp.bitwise_xor(tensor_index, mask) * heads_here
        for kind, cache in enumerate((keys_ref, values_ref)):
            for row in range(rows_dev):
                start = (kind * rows_dev + row) * heads_here
                moves.append((cache.at[row, pl.ds(head, heads_here)], far.at[pl.ds(start, heads_here)]))
    moves.append((b_query_ref, factors_ref.at[:, pl.ds(0, wide)]))
    for place, ref in enumerate((b_key_ref, b_value_ref)):
        moves.append((ref, factors_ref.at[pl.ds(place * narrow, narrow), pl.ds(wide, rank)]))
    for piece in range(a_out_ref.shape[0] // rank):
        moves.append(
            (
                a_out_ref.at[pl.ds(piece * rank, rank)],
                factors_ref.at[:, pl.ds(wide + (piece + 1) * rank, rank)],
            )
        )
    moves = begun(2, moves)
    for copy in inputs[:3]:
        copy.wait()
    rows, width = first_ref.shape
    pieces = []
    sums = [jnp.zeros((rows, 128), F32), jnp.zeros((rows, 128), F32)]

    def by_owner(pair):
        ordered = []
        for owner in range(rows // rows_dev):
            for part in pair:
                ordered.append(part[owner * rows_dev : (owner + 1) * rows_dev])
        return jnp.concatenate(ordered, axis=0)

    for piece in range(width // 128):
        columns = slice(piece * 128, (piece + 1) * 128)
        steps = [hidden[step, :, columns].astype(F32) for step in range(2)]
        sums = [total + step * step for total, step in zip(sums, steps)]
        gain = gain_held[piece : piece + 1, :].astype(F32)
        scaled_ref[:, columns] = by_owner([step * gain for step in steps]).astype(BF16)
    squares_ref[...] = by_owner(sums)
    for copy in inputs[3:]:
        copy.wait()
    depth = a_query_ref.shape[0]
    own = scaled_ref[:, aligned(tensor_index * depth, depth, 128)]
    start = 2 * rows_dev * heads_here
    low_rows = scaled_ref.shape[0]
    for place in range(3):
        low = jnp.dot(own, a_held[place], preferred_element_type=F32)
        low_ref[:, place * rank : (place + 1) * rank] = low
        for far in (far_1, far_2, far_3):
            far[start + place, :low_rows, :] = low.astype(BF16)
    for copy in moves:
        copy.wait()


def project_body(
    rows_dev,
    lengths_ref,
    scaled_ref,
    query_ref,
    key_ref,
    value_ref,
    sums_ref,
    trig_ref,
    length_ref,
    ring,
    key_held,
    value_held,
    lengths_held,
    ring_sem,
    held_sem,
):
    slots, depth, columns = ring.shape
    chunks = query_ref.shape[0] // depth

    def fetch(chunk):
        slot = chunk % slots
        return pltpu.make_async_copy(
            query_ref.at[pl.ds(chunk * depth, depth)], ring.at[slot], ring_sem.at[slot]
        )

    side = [
        pltpu.make_async_copy(key_ref, key_held, held_sem.at[0]),
        pltpu.make_async_copy(value_ref, value_held, held_sem.at[1]),
    ]
    for chunk in range(min(slots, chunks)):
        fetch(chunk).start()
    for copy in side:
        copy.start()
    lengths_copy = pltpu.make_async_copy(lengths_ref, lengths_held, held_sem.at[2])
    lengths_copy.start()
    lengths_copy.wait()
    shape = length_ref.shape
    half = shape[1] // 2
    row = lax.broadcasted_iota(jnp.int32, shape, 0)
    lane = lax.broadcasted_iota(jnp.int32, shape, 1)
    length = jnp.zeros(shape, jnp.int32)
    for place in range(rows_dev):
        length = length + jnp.where(row % rows_dev == place, lengths_held[place], 0)
    length_ref[...] = length
    exponent = (lane % half).astype(F32) / half
    frequency = jnp.exp(exponent * (-math.log(ROPE_BASE)))
    angles = (length + row // rows_dev).astype(F32) * frequency
    sine = jnp.sin(angles)
    trig_ref[: shape[0], :] = jnp.cos(angles)
    trig_ref[shape[0] :, :] = jnp.where(lane < half, -sine, sine)
    for chunk in range(chunks):
        fetch(chunk).wait()
        term = jnp.dot(
            scaled_ref[:, chunk * depth : (chunk + 1) * depth],
            ring[chunk % slots],
            preferred_element_type=F32,
        )
        if chunk == 0:
            sums_ref[:, :columns] = term
        else:
            sums_ref[:, :columns] += term
        if chunk + slots < chunks:
            fetch(chunk + slots).start()
    place = columns
    for copy, held in zip(side, (key_held, value_held)):
        copy.wait()
        sums_ref[:, place : place + held.shape[1]] = jnp.dot(
            scaled_ref[...], held[...], preferred_element_type=F32
        )
        place += held.shape[1]


def first_send_body(sums_ref, low_ref, squares_ref, far_1, far_2, far_3, send_ref, keep_ref, full):
    core = lax.rem(lax.axis_index("dp"), 2)
    columns = sums_ref.shape[1]
    rows, low_columns = low_ref.shape
    rank = low_columns // 3
    full[:, :columns] = sums_ref[...]
    for place in range(3):
        low = low_ref[:, place * rank : (place + 1) * rank]
        for far in (far_1, far_2, far_3):
            low = low + far[far.shape[0] - 3 + place, :rows, :].astype(F32)
        full[:, columns + place * rank : columns + (place + 1) * rank] = low
    full[:, columns + low_columns :] = split_sum(
        jnp.sum(squares_ref[...], axis=1, keepdims=True), 128
    )
    share = rows // 4
    other = 1 - core
    send_ref[...] = jnp.concatenate(
        [
            full[aligned(other * share, share, 8), :],
            full[aligned((other + 2) * share, share, 8), :],
        ],
        axis=0,
    ).astype(BF16)
    keep_ref[:share, :] = full[aligned(core * share, share, 8), :]
    keep_ref[share:, :] = full[aligned((core + 2) * share, share, 8), :]


def second_send_body(keep_ref, arrived_ref, send_ref, kept_ref, full):
    chip = lax.axis_index("dp") // 2
    full[...] = keep_ref[...] + arrived_ref[...].astype(F32)
    full[:, -128:] = split_sum(jnp.sum(full[:, -128:], axis=1, keepdims=True), 128)
    share = full.shape[0] // 2
    send_ref[...] = full[aligned((1 - chip) * share, share, 8), :].astype(BF16)
    kept_ref[...] = full[aligned(chip * share, share, 8), :]


def attend_body(
    rows_dev,
    length_ref,
    trig_ref,
    kept_ref,
    arrived_ref,
    factors_0,
    factors_1,
    factors_2,
    factors_3,
    near,
    far_1,
    far_2,
    far_3,
    heads_ref,
    low_query,
    low_narrow,
    turned,
    mixed,
    keys_all,
    values_all,
):
    dp_index = lax.axis_index("dp")
    tensor_index = lax.axis_index("tensor")
    rows = 2 * rows_dev
    span, head_dim = near.shape[1:]
    key_heads = keys_all.shape[0] // rows_dev
    query_columns = heads_ref.shape[1]
    heads = query_columns // head_dim
    group = heads // key_heads
    sources = lax.axis_size("tensor")
    rank = factors_0.shape[0]
    owners = lax.axis_size("dp")
    wide = query_columns // owners
    narrow = key_heads * head_dim // owners

    for place in range(rows_dev * key_heads):
        for mask, block in enumerate((near, far_1, far_2, far_3)):
            rows_here = slice(mask * span, (mask + 1) * span)
            keys_all[place, rows_here, :] = block[place]
            values_all[place, rows_here, :] = block[rows_dev * key_heads + place]

    total = kept_ref[...] + arrived_ref[...].astype(F32)
    joint = query_columns + 2 * key_heads * head_dim
    squares = jnp.sum(total[:, -128:], axis=1, keepdims=True)
    scale = lax.rsqrt(squares / D + EPS)
    lows = [
        total[:, joint + place * rank : joint + (place + 1) * rank].astype(BF16)
        for place in range(3)
    ]
    for mask, factors in enumerate((factors_0, factors_1, factors_2, factors_3)):
        owner = jnp.bitwise_xor(dp_index, mask)
        low_query[owner] = jnp.dot(lows[0], factors[:, :wide], preferred_element_type=F32)
        pair = factors[:, wide : wide + 2 * narrow]
        for place in range(2):
            low_narrow[place, owner] = lax.dot_general(
                lows[place + 1], pair, (((1,), (1,)), ((), ())), preferred_element_type=F32
            )
    cosine = trig_ref[:rows, :]
    sine = trig_ref[rows:, :]

    def turn(vector):
        return vector * cosine + pltpu.roll(vector, head_dim // 2, 1) * sine

    def rounded(vector):
        return vector.astype(BF16).astype(F32)

    for head in range(heads):
        column = head * head_dim
        owner, inner = column // wide, column % wide
        vector = (
            total[:, column : column + head_dim]
            + ADAPTER_SCALE * low_query[owner, :, inner : inner + head_dim]
        )
        start = (head % group) * rows
        turned[head // group, start : start + rows, :] = turn(rounded(vector * scale))

    lane = lax.broadcasted_iota(jnp.int32, (rows, head_dim), 1)
    per_head = head_dim // narrow
    fresh = [[], []]
    for place in range(2):
        for head in range(key_heads):
            low = jnp.zeros((rows, head_dim), F32)
            for part in range(per_head):
                piece = low_narrow[place, head * per_head + part]
                shift = (part * narrow - place * narrow) % (2 * narrow)
                if shift:
                    piece = pltpu.roll(piece, shift, 1)
                low = jnp.where(lane // narrow == part, piece, low)
            column = query_columns + place * key_heads * head_dim + head * head_dim
            vector = rounded(
                (total[:, column : column + head_dim] + ADAPTER_SCALE * low) * scale
            )
            fresh[place].append(turn(vector) if place == 0 else vector)

    cached = sources * span
    width = keys_all.shape[1]
    column = lax.broadcasted_iota(jnp.int32, (1, width), 1)
    position = jnp.where(column == cached, -1, 1 << 30)
    for mask in range(sources):
        base = jnp.bitwise_xor(tensor_index, mask) * span
        inside = (column >= mask * span) & (column < (mask + 1) * span)
        position = jnp.where(inside, column - mask * span + base, position)
    step = lax.broadcasted_iota(jnp.int32, (2 * group, width), 0) % 2
    second = (step == 1) & (
        lax.broadcasted_iota(jnp.int32, (2 * group, width), 1) == cached + 1
    )
    score_scale = 1.0 / math.sqrt(head_dim)
    for row in range(rows_dev):
        valid = (position < length_ref[row : row + 1, :1]) | second
        for head in range(key_heads):
            place = row * key_heads + head
            for joined, parts in ((keys_all, fresh[0]), (values_all, fresh[1])):
                joined[place, cached:, :] = jnp.concatenate(
                    [
                        parts[head][row : row + 1],
                        parts[head][rows_dev + row : rows_dev + row + 1],
                        jnp.zeros((width - cached - 2, head_dim), F32),
                    ],
                    axis=0,
                ).astype(BF16)
            query = turned[head, pl.ds(row, 2 * group, stride=rows_dev), :].astype(BF16)
            scores = (
                lax.dot_general(
                    query,
                    keys_all[place],
                    (((1,), (1,)), ((), ())),
                    preferred_element_type=F32,
                )
                * score_scale
            )
            scores = jnp.where(valid, scores, MASKED_FILLER)
            highest = jnp.max(scores, axis=1, keepdims=True)
            weights = jnp.where(valid, jnp.exp(scores - highest), 0.0)
            totals = jnp.sum(weights, axis=1, keepdims=True)
            weighted = jnp.dot(
                weights.astype(BF16), values_all[place], preferred_element_type=F32
            )
            mixed[head, pl.ds(row, 2 * group, stride=rows_dev), :] = weighted / totals
    for head in range(heads):
        start = (head % group) * rows
        heads_ref[:, head * head_dim : (head + 1) * head_dim] = mixed[
            head // group, start : start + rows, :
        ].astype(BF16)


def output_body(
    heads_0,
    heads_1,
    heads_2,
    heads_3,
    factors_0,
    factors_1,
    factors_2,
    factors_3,
    weight_ref,
    send_1,
    send_2,
    send_3,
    keep_ref,
    wide_rows,
    all_rows,
    sums,
    ring,
    ring_sem,
):
    dp_index = lax.axis_index("dp")
    tensor_index = lax.axis_index("tensor")
    slots, depth, columns = ring.shape
    chunks = weight_ref.shape[0] // depth

    def fetch(chunk):
        slot = chunk % slots
        return pltpu.make_async_copy(
            weight_ref.at[pl.ds(chunk * depth, depth)], ring.at[slot], ring_sem.at[slot]
        )

    for chunk in range(min(slots, chunks)):
        fetch(chunk).start()
    share = heads_0.shape[0]
    for mask, part in enumerate((heads_0, heads_1, heads_2, heads_3)):
        owner = jnp.bitwise_xor(dp_index, mask)
        wide_rows[aligned(owner * share, share, 8), :] = part[...].astype(F32)
    all_rows[...] = wide_rows[...].astype(BF16)
    rank = factors_0.shape[0]
    block = all_rows.shape[1] // lax.axis_size("dp")
    pieces = block // rank
    base = factors_0.shape[1] - pieces * rank
    low = jnp.zeros((all_rows.shape[0], rank), F32)
    for mask, factors in enumerate((factors_0, factors_1, factors_2, factors_3)):
        owner = jnp.bitwise_xor(dp_index, mask)
        for piece in range(pieces):
            low = low + jnp.dot(
                all_rows[:, aligned(owner * block + piece * rank, rank, 128)],
                factors[:, base + piece * rank : base + (piece + 1) * rank],
                preferred_element_type=F32,
            )
    for chunk in range(chunks):
        fetch(chunk).wait()
        term = jnp.dot(
            all_rows[:, chunk * depth : (chunk + 1) * depth],
            ring[chunk % slots],
            preferred_element_type=F32,
        )
        if chunk == 0:
            sums[...] = term
        else:
            sums[...] += term
        if chunk + slots < chunks:
            fetch(chunk + slots).start()
    part = columns // lax.axis_size("tensor")
    for mask, send in ((1, send_1), (2, send_2), (3, send_3)):
        target = jnp.bitwise_xor(tensor_index, mask)
        send[:, :part] = sums[:, aligned(target * part, part, 128)].astype(BF16)
        send[:, part:] = low.astype(BF16)
    keep_ref[:, :part] = sums[:, aligned(tensor_index * part, part, 128)]
    keep_ref[:, part:] = low


def finish_body(rows_dev, keep_ref, far_1, far_2, far_3, b_out_ref, part_ref):
    total = keep_ref[...]
    for far in (far_1, far_2, far_3):
        total = total + far[...].astype(F32)
    part = b_out_ref.shape[1]
    low = total[:, part:].astype(BF16)
    result = total[:, :part] + ADAPTER_SCALE * jnp.dot(
        low, b_out_ref[...], preferred_element_type=F32
    )
    pieces = []
    for step in range(2):
        for owner in range(result.shape[0] // (2 * rows_dev)):
            start = (2 * owner + step) * rows_dev
            pieces.append(result[start : start + rows_dev])
    part_ref[...] = jnp.concatenate(pieces, axis=0).astype(BF16)


def place_body(part_0, part_1, part_2, part_3, first_ref, second_ref, sems):
    tensor_index = lax.axis_index("tensor")
    rows = first_ref.shape[0]
    copies = []
    for mask, part in enumerate((part_0, part_1, part_2, part_3)):
        width = part.shape[1]
        columns = aligned(jnp.bitwise_xor(tensor_index, mask) * width, width, 128)
        for step, target in enumerate((first_ref, second_ref)):
            copies.append(
                pltpu.make_async_copy(
                    part.at[pl.ds(step * rows, rows)],
                    target.at[:, columns],
                    sems.at[mask, step],
                )
            )
    for copy in copies:
        copy.start()
    for copy in copies:
        copy.wait()


def on_device_joined(
    hidden_first,
    hidden_second,
    norm_gain,
    query_weight,
    w_key,
    w_value,
    w_out,
    a_query,
    b_query,
    a_key,
    b_key,
    a_value,
    b_value,
    a_out,
    b_out,
    cache_keys,
    cache_values,
    lengths,
):
    shape = jax.ShapeDtypeStruct
    rows, width = hidden_first.shape
    rows_dev, all_key_heads, span, head_dim = cache_keys.shape
    n_tensor = lax.axis_size("tensor")
    key_heads = all_key_heads // n_tensor
    rank = a_query.shape[1]
    query_columns = query_weight.shape[1]
    key_columns = w_key.shape[1]
    joint = query_columns + 2 * key_columns
    both = 2 * rows
    share = 2 * rows_dev
    low_columns = 3 * rank
    blocks = 2 * rows_dev * key_heads
    pack_columns = b_query.shape[1] + rank + a_out.shape[0]

    scaled, squares, low, near, far_1, far_2, far_3, factors = kernel_call(
        functools.partial(prepare_body, rows_dev),
        (
            shape((both, width), BF16),
            shape((both, 128), F32),
            shape((both, low_columns), F32),
            shape((blocks, span, head_dim), BF16),
            shape((blocks + 3, span, head_dim), BF16),
            shape((blocks + 3, span, head_dim), BF16),
            shape((blocks + 3, span, head_dim), BF16),
            shape((rank, pack_columns), BF16),
        ),
        [hbm_spec()] * 12,
        [
            pltpu.VMEM((2, rows, width), BF16),
            pltpu.VMEM((width // 128, 128), BF16),
            pltpu.VMEM((3,) + a_query.shape, BF16),
            pltpu.SemaphoreType.DMA((3,)),
        ],
        moved=6e6,
    )(
        *in_hbm(
            hidden_first,
            hidden_second,
            norm_gain.reshape(width // 128, 128),
            a_query,
            a_key,
            a_value,
            cache_keys,
            cache_values,
            b_query,
            b_key.T,
            b_value.T,
            a_out,
        )
    )
    far = [swapped(part, "tensor", mask) for mask, part in ((1, far_1), (2, far_2), (3, far_3))]
    factors_x = swapped(factors, "dp", 2)
    factors_core = swapped(factors, "dp", 1)

    depth = math.gcd(width, 256)
    sums, trig, length = kernel_call(
        functools.partial(project_body, rows_dev),
        (
            shape((both, joint), F32),
            shape((2 * share, head_dim), F32),
            shape((share, head_dim), jnp.int32),
        ),
        [hbm_spec(), vmem_spec(), hbm_spec(), hbm_spec(), hbm_spec()],
        [
            pltpu.VMEM((4, depth, query_columns), BF16),
            pltpu.VMEM((width, key_columns), BF16),
            pltpu.VMEM((width, key_columns), BF16),
            pltpu.SMEM((rows_dev,), jnp.int32),
            pltpu.SemaphoreType.DMA((4,)),
            pltpu.SemaphoreType.DMA((3,)),
        ],
        moved=2 * width * joint,
    )(*in_hbm(lengths), scaled, *in_hbm(query_weight, w_key, w_value))
    extended = joint + low_columns + 128
    send, keep = kernel_call(
        first_send_body,
        (shape((rows, extended), BF16), shape((rows, extended), F32)),
        [vmem_spec()] * 6,
        [pltpu.VMEM((both, extended), F32)],
    )(sums, low, squares, *far)
    factors_x, send = lax.optimization_barrier((factors_x, send))
    arrived = swapped(send, "dp", 1)
    factors_both = swapped(factors_x, "dp", 1)
    all_factors = (factors, factors_core, factors_x, factors_both)
    send, kept = kernel_call(
        second_send_body,
        (shape((share, extended), BF16), shape((share, extended), F32)),
        [vmem_spec()] * 2,
        [pltpu.VMEM((rows, extended), F32)],
    )(keep, arrived)
    arrived = swapped(send, "dp", 2)
    heads_here = query_columns // head_dim
    group = heads_here // key_heads
    positions = n_tensor * span + 16
    owners = lax.axis_size("dp")
    (heads,) = kernel_call(
        functools.partial(attend_body, rows_dev),
        (shape((share, query_columns), BF16),),
        [vmem_spec()] * 12,
        [
            pltpu.VMEM((owners, share, query_columns // owners), F32),
            pltpu.VMEM((2, owners, share, 2 * key_columns // owners), F32),
            pltpu.VMEM((key_heads, group * share, head_dim), F32),
            pltpu.VMEM((key_heads, group * share, head_dim), F32),
            pltpu.VMEM((rows_dev * key_heads, positions, head_dim), BF16),
            pltpu.VMEM((rows_dev * key_heads, positions, head_dim), BF16),
        ],
        moved=10e6,
    )(length, trig, kept, arrived, *all_factors, near, *far)

    heads_x = swapped(heads, "dp", 2)
    heads_core = swapped(heads, "dp", 1)
    heads_both = swapped(heads_x, "dp", 1)
    out_columns = w_out.shape[1]
    part = out_columns // n_tensor
    depth = math.gcd(w_out.shape[0], 256)
    send_1, send_2, send_3, keep = kernel_call(
        output_body,
        (
            shape((both, part + rank), BF16),
            shape((both, part + rank), BF16),
            shape((both, part + rank), BF16),
            shape((both, part + rank), F32),
        ),
        [vmem_spec()] * 8 + [hbm_spec()],
        [
            pltpu.VMEM((both, w_out.shape[0]), F32),
            pltpu.VMEM((both, w_out.shape[0]), BF16),
            pltpu.VMEM((both, out_columns), F32),
            pltpu.VMEM((4, depth, out_columns), BF16),
            pltpu.SemaphoreType.DMA((4,)),
        ],
        moved=2 * w_out.size,
    )(heads, heads_core, heads_x, heads_both, *all_factors, *in_hbm(w_out))
    far = [swapped(block, "tensor", mask) for mask, block in ((1, send_1), (2, send_2), (3, send_3))]
    (done,) = kernel_call(
        functools.partial(finish_body, rows_dev),
        (shape((both, part), BF16),),
        [vmem_spec()] * 5,
    )(keep, *far, b_out)
    parts = [done] + [swapped(done, "tensor", mask) for mask in (1, 2, 3)]
    return kernel_call(
        place_body,
        (shape((rows, out_columns), BF16), shape((rows, out_columns), BF16)),
        [vmem_spec()] * 4,
        [pltpu.SemaphoreType.DMA((4, 2))],
        out_specs=(hbm_spec(), hbm_spec()),
    )(*parts)


def takes_joined(mesh):
    return mesh.shape["dp"] == 4 and mesh.shape["tensor"] == 4


def solution(mesh):
    in_specs = (
        P("groups", "dp"),
        P("groups", "dp"),
        P("dp"),
        P("dp", "tensor"),
        P("dp", "tensor"),
        P("dp", "tensor"),
        P("tensor", "dp"),
        P(("dp", "tensor"), None),
        P(None, ("tensor", "dp")),
        P(("dp", "tensor"), None),
        P(None, ("tensor", "dp")),
        P(("dp", "tensor"), None),
        P(None, ("tensor", "dp")),
        P(("tensor", "dp"), None),
        P(None, ("dp", "tensor")),
        P(("groups", "dp"), None, "tensor", None),
        P(("groups", "dp"), None, "tensor", None),
        P(("groups", "dp")),
    )
    out_specs = (P("groups", "dp"), P("groups", "dp"))
    return jax.shard_map(
        on_device_joined if takes_joined(mesh) else on_device,
        mesh=mesh,
        in_specs=in_specs,
        out_specs=out_specs,
        check_vma=False,
    )
```

```python
import functools
import math

import jax
import jax.numpy as jnp
import numpy as np
from jax import lax
from jax.experimental import pallas as pl
from jax.experimental.pallas import tpu as pltpu
from jax.sharding import PartitionSpec as P

D = 16384


ADAPTER_SCALE = 2.0
ROPE_BASE = 500000.0
EPS = 1e-05
MASKED_FILLER = -1e30
BF16 = jnp.bfloat16
F32 = jnp.float32


def joined_2(part, axis, combine):
    gathered = jax.tree.map(lambda a: lax.all_gather(a, axis), part)

    def take(source):
        return jax.tree.map(lambda a: lax.dynamic_index_in_dim(a, source, 0, False), gathered)

    return lax.fori_loop(
        1, lax.axis_size(axis), lambda source, state: combine(state, take(source)), take(0)
    )


def merge_weight(frozen_weight, factor_in, factor_out):
    adapter_update = jnp.dot(factor_in, factor_out, preferred_element_type=jnp.float32)
    return (frozen_weight.astype(jnp.float32) + ADAPTER_SCALE * adapter_update).astype(jnp.bfloat16)


def rotary(vectors, positions_now):
    half_dim = vectors.shape[-1] // 2
    frequency = ROPE_BASE ** (-jnp.arange(half_dim, dtype=jnp.float32) / half_dim)
    angles = positions_now.astype(jnp.float32)[:, None] * frequency[None, :]
    cosine = jnp.cos(angles)[:, None, :]
    sine_part = jnp.sin(angles)[:, None, :]
    lower = vectors[..., :half_dim]
    upper = vectors[..., half_dim:]
    return jnp.concatenate(
        [lower * cosine - upper * sine_part, upper * cosine + lower * sine_part], axis=-1
    )


def combine_partial(earlier, later):
    highest = jnp.maximum(earlier[0], later[0])
    weight_a = jnp.exp(earlier[0] - highest)
    weight_b = jnp.exp(later[0] - highest)
    return (
        highest,
        earlier[1] * weight_a + later[1] * weight_b,
        earlier[2] * weight_a[..., None] + later[2] * weight_b[..., None],
    )


def on_device(
    hidden_first,
    hidden_second,
    norm_gain,
    query_weight,
    w_key,
    w_value,
    w_out,
    a_query,
    b_query,
    a_key,
    b_key,
    a_value,
    b_value,
    a_out,
    b_out,
    cache_keys,
    cache_values,
    lengths,
):
    tensor_parts = (
        lax.all_gather(a_query, "tensor", axis=0, tiled=True),
        lax.all_gather(a_key, "tensor", axis=0, tiled=True),
        lax.all_gather(a_value, "tensor", axis=0, tiled=True),
        lax.all_gather(b_out, "tensor", axis=1, tiled=True),
    )
    data_parts = (
        lax.all_gather(b_query, "dp", axis=1, tiled=True),
        lax.all_gather(b_key, "dp", axis=1, tiled=True),
        lax.all_gather(b_value, "dp", axis=1, tiled=True),
        lax.all_gather(a_out, "dp", axis=0, tiled=True),
    )
    merged_qkv = jnp.concatenate(
        [
            merge_weight(query_weight, tensor_parts[0], data_parts[0]),
            merge_weight(w_key, tensor_parts[1], data_parts[1]),
            merge_weight(w_value, tensor_parts[2], data_parts[2]),
        ],
        axis=1,
    )
    merged_output = merge_weight(w_out, data_parts[3], tensor_parts[3])
    n_tensor = lax.axis_size("tensor")
    tensor_index = lax.axis_index("tensor")
    rows_dev, key_value_heads, cache_span, head_dim = cache_keys.shape
    query_cols = query_weight.shape[1]
    key_cols = w_key.shape[1]
    joint_cols = query_cols + 2 * key_cols
    heads_here = query_cols // head_dim
    all_heads = heads_here * n_tensor
    group_size = all_heads // key_value_heads
    score_scale = 1.0 / math.sqrt(head_dim)
    cache_positions = tensor_index * cache_span + jnp.arange(cache_span, dtype=jnp.int32)
    cache_valid = cache_positions[None, :] < lengths[:, None]
    first_owner = tensor_index == 0
    fresh_keys = []
    fresh_values = []
    results = []
    for step_index, hidden in enumerate((hidden_first, hidden_second)):
        values_f = hidden.astype(jnp.float32)
        squares = lax.psum(jnp.sum(values_f * values_f, axis=1), "dp")
        normed = (
            values_f * lax.rsqrt(squares / D + EPS)[:, None] * norm_gain.astype(jnp.float32)
        ).astype(jnp.bfloat16)
        projected = lax.psum_scatter(
            jnp.dot(normed, merged_qkv, preferred_element_type=jnp.float32),
            "dp",
            scatter_dimension=0,
            tiled=True,
        ).astype(jnp.bfloat16)
        joined = lax.all_gather(projected, "tensor", axis=1, tiled=True).reshape(
            rows_dev, n_tensor, joint_cols
        )
        queries = joined[:, :, :query_cols].reshape(rows_dev, all_heads, head_dim)
        key_now = joined[:, :, query_cols : query_cols + key_cols].reshape(
            rows_dev, key_value_heads, head_dim
        )
        value_now = joined[:, :, query_cols + key_cols :].reshape(
            rows_dev, key_value_heads, head_dim
        )
        positions_now = lengths + step_index
        queries = rotary(queries.astype(jnp.float32), positions_now).astype(jnp.bfloat16)
        queries = queries.reshape(rows_dev, key_value_heads, group_size, head_dim)
        fresh_keys.append(rotary(key_now.astype(jnp.float32), positions_now).astype(jnp.bfloat16))
        fresh_values.append(value_now)
        cache_scores = (
            jnp.einsum("rkgd,rksd->rkgs", queries, cache_keys, preferred_element_type=jnp.float32)
            * score_scale
        )
        cache_scores = jnp.where(cache_valid[:, None, None, :], cache_scores, MASKED_FILLER)
        new_scores = (
            jnp.einsum(
                "rkgd,rknd->rkgn",
                queries,
                jnp.stack(fresh_keys, axis=2),
                preferred_element_type=jnp.float32,
            )
            * score_scale
        )
        new_scores = jnp.where(first_owner, new_scores, MASKED_FILLER)
        highest = jnp.maximum(jnp.max(cache_scores, axis=-1), jnp.max(new_scores, axis=-1))
        cache_weights = jnp.where(
            cache_valid[:, None, None, :], jnp.exp(cache_scores - highest[..., None]), 0.0
        )
        new_weights = jnp.where(first_owner, jnp.exp(new_scores - highest[..., None]), 0.0)
        totals = jnp.sum(cache_weights, axis=-1) + jnp.sum(new_weights, axis=-1)
        weighted = jnp.einsum(
            "rkgs,rksd->rkgd", cache_weights, cache_values, preferred_element_type=jnp.float32
        )
        weighted = weighted + jnp.einsum(
            "rkgn,rknd->rkgd",
            new_weights,
            jnp.stack(fresh_values, axis=2),
            preferred_element_type=jnp.float32,
        )
        highest = highest.reshape(rows_dev, all_heads)
        totals = totals.reshape(rows_dev, all_heads)
        weighted = weighted.reshape(rows_dev, all_heads, head_dim)
        high_all, total_all, weighted_all = joined_2(
            (highest, totals, weighted), "tensor", combine_partial
        )
        normalized = weighted_all / total_all[..., None]
        own_heads = lax.dynamic_slice_in_dim(normalized, tensor_index * heads_here, heads_here, 1)
        heads = own_heads.reshape(rows_dev, query_cols).astype(jnp.bfloat16)
        out_terms = jnp.dot(
            lax.all_gather(heads, "dp", axis=0, tiled=True),
            merged_output,
            preferred_element_type=jnp.float32,
        )
        attn_out = lax.psum(out_terms, "tensor").astype(jnp.bfloat16)
        results.append(attn_out)
    return (results[0], results[1])

def swapped(array, axis, mask):
    size = lax.axis_size(axis)
    return lax.ppermute(array, axis, [(k, k ^ mask) for k in range(size)])


def vmem_spec():
    return pl.BlockSpec(memory_space=pltpu.VMEM)


def any_spec():
    return pl.BlockSpec(memory_space=pl.ANY)


def hbm_spec():
    return pl.BlockSpec(memory_space=pltpu.HBM)


def in_hbm(*arrays):
    return [pltpu.with_memory_space_constraint(array, pltpu.HBM) for array in arrays]


def cost(moved):
    return pl.CostEstimate(flops=0, bytes_accessed=int(moved), transcendentals=0)


def kernel_call(body, outs, in_specs, scratch=(), mib=12, out_specs=None, moved=0):
    return pl.pallas_call(
        body,
        out_shape=outs,
        in_specs=in_specs,
        out_specs=out_specs or tuple(vmem_spec() for _ in outs),
        scratch_shapes=list(scratch),
        cost_estimate=cost(moved),
        compiler_params=pltpu.CompilerParams(vmem_limit_bytes=mib << 20),
    )


def aligned(start, size, unit):
    return pl.ds(pl.multiple_of(start, unit), size)


def split_sum(total, width):
    high = total.astype(BF16).astype(F32)
    rest = total - high
    middle = rest.astype(BF16).astype(F32)
    low = rest - middle
    lane = lax.broadcasted_iota(jnp.int32, (total.shape[0], width), 1)
    return jnp.where(
        lane == 0, high, jnp.where(lane == 1, middle, jnp.where(lane == 2, low, 0.0))
    )


def low_places(shape, rows, place):
    blocks, span, _ = shape
    first = blocks - -(-3 * rows // span)
    for part in range(0, rows, 16):
        flat = place * rows + part
        yield first + flat // span, flat % span, part


def prepare_body(
    rows_dev,
    first_ref,
    second_ref,
    gain_ref,
    a_query_ref,
    a_key_ref,
    a_value_ref,
    keys_ref,
    values_ref,
    b_query_ref,
    b_key_ref,
    b_value_ref,
    a_out_ref,
    scaled_ref,
    squares_ref,
    low_ref,
    near,
    far_1,
    far_2,
    far_3,
    far_values,
    factors_ref,
    hidden,
    gain_held,
    a_held,
    sems,
):
    tensor_index = lax.axis_index("tensor")
    heads_here = keys_ref.shape[1] // lax.axis_size("tensor")
    rank = a_query_ref.shape[1]
    wide = b_query_ref.shape[1]
    narrow = b_key_ref.shape[0]

    def begun(group, pairs):
        copies = [pltpu.make_async_copy(*pair, sems.at[group]) for pair in pairs]
        for copy in copies:
            copy.start()
        return copies

    inputs = begun(
        0, [(first_ref, hidden.at[0]), (second_ref, hidden.at[1]), (gain_ref, gain_held)]
    )
    inputs += begun(
        1,
        [(ref, a_held.at[place]) for place, ref in enumerate((a_query_ref, a_key_ref, a_value_ref))],
    )
    moves = []
    for mask, far in enumerate((near, far_1, far_2, far_3)):
        head = jnp.bitwise_xor(tensor_index, mask) * heads_here
        for kind, cache in enumerate((keys_ref, values_ref)):
            late = mask == 3 and kind == 1
            for row in range(rows_dev):
                start = (row if late else kind * rows_dev + row) * heads_here
                target = far_values if late else far
                moves.append(
                    (cache.at[row, pl.ds(head, heads_here)], target.at[pl.ds(start, heads_here)])
                )
    moves.append((b_query_ref, factors_ref.at[:, pl.ds(0, wide)]))
    for place, ref in enumerate((b_key_ref, b_value_ref)):
        moves.append((ref, factors_ref.at[pl.ds(place * narrow, narrow), pl.ds(wide, rank)]))
    for piece in range(a_out_ref.shape[0] // rank):
        moves.append(
            (
                a_out_ref.at[pl.ds(piece * rank, rank)],
                factors_ref.at[:, pl.ds(wide + (piece + 1) * rank, rank)],
            )
        )
    moves = begun(2, moves)
    @pl.when(tensor_index >= 0)
    def scaled():
        for copy in inputs[:3]:
            copy.wait()
        rows, width = first_ref.shape
        pieces = []
        sums = [jnp.zeros((rows, 128), F32), jnp.zeros((rows, 128), F32)]

        def by_owner(pair):
            ordered = []
            for owner in range(rows // rows_dev):
                for part in pair:
                    ordered.append(part[owner * rows_dev : (owner + 1) * rows_dev])
            return jnp.concatenate(ordered, axis=0)

        for piece in range(width // 128):
            columns = slice(piece * 128, (piece + 1) * 128)
            steps = [hidden[step, :, columns].astype(F32) for step in range(2)]
            sums = [total + step * step for total, step in zip(sums, steps)]
            gain = gain_held[piece : piece + 1, :].astype(F32)
            scaled_ref[:, columns] = by_owner([step * gain for step in steps]).astype(BF16)
        squares_ref[...] = by_owner(sums)
        for copy in inputs[3:]:
            copy.wait()
        depth = a_query_ref.shape[0]
        own = scaled_ref[:, aligned(tensor_index * depth, depth, 128)]
        low_rows = scaled_ref.shape[0]
        for place in range(3):
            low = jnp.dot(own, a_held[place], preferred_element_type=F32)
            low_ref[:, place * rank : (place + 1) * rank] = low
            for far in (far_1, far_2, far_3):
                for at, row, part in low_places(far.shape, low_rows, place):
                    far[at, row : row + 16, :] = low[part : part + 16].astype(BF16)

    for copy in moves:
        copy.wait()


def project_body(
    rows_dev,
    lengths_ref,
    scaled_ref,
    query_ref,
    key_ref,
    value_ref,
    sums_ref,
    trig_ref,
    length_ref,
    ring,
    key_held,
    value_held,
    lengths_held,
    ring_sem,
    held_sem,
):
    slots, depth, columns = ring.shape
    chunks = query_ref.shape[0] // depth

    def fetch(chunk):
        slot = chunk % slots
        return pltpu.make_async_copy(
            query_ref.at[pl.ds(chunk * depth, depth)], ring.at[slot], ring_sem.at[slot]
        )

    side = [
        pltpu.make_async_copy(key_ref, key_held, held_sem.at[0]),
        pltpu.make_async_copy(value_ref, value_held, held_sem.at[1]),
    ]
    for copy in side:
        copy.start()
    for chunk in range(min(slots, chunks)):
        fetch(chunk).start()
    lengths_copy = pltpu.make_async_copy(lengths_ref, lengths_held, held_sem.at[2])
    lengths_copy.start()
    lengths_copy.wait()
    shape = length_ref.shape
    half = shape[1] // 2
    row = lax.broadcasted_iota(jnp.int32, shape, 0)
    lane = lax.broadcasted_iota(jnp.int32, shape, 1)
    length = jnp.zeros(shape, jnp.int32)
    for place in range(rows_dev):
        length = length + jnp.where(row % rows_dev == place, lengths_held[place], 0)
    length_ref[...] = length
    exponent = (lane % half).astype(F32) / half
    frequency = jnp.exp(exponent * (-math.log(ROPE_BASE)))
    angles = (length + row // rows_dev).astype(F32) * frequency
    sine = jnp.sin(angles)
    trig_ref[: shape[0], :] = jnp.cos(angles)
    trig_ref[shape[0] :, :] = jnp.where(lane < half, -sine, sine)
    place = columns
    for copy, held in zip(side, (key_held, value_held)):
        copy.wait()
        sums_ref[:, place : place + held.shape[1]] = jnp.dot(
            scaled_ref[...], held[...], preferred_element_type=F32
        )
        place += held.shape[1]
    for chunk in range(chunks):
        fetch(chunk).wait()
        term = jnp.dot(
            scaled_ref[:, chunk * depth : (chunk + 1) * depth],
            ring[chunk % slots],
            preferred_element_type=F32,
        )
        if chunk == 0:
            sums_ref[:, :columns] = term
        else:
            sums_ref[:, :columns] += term
        if chunk + slots < chunks:
            fetch(chunk + slots).start()


def first_send_body(sums_ref, low_ref, squares_ref, far_1, far_2, far_3, send_ref, keep_ref, full):
    core = lax.rem(lax.axis_index("dp"), 2)
    columns = sums_ref.shape[1]
    rows, low_columns = low_ref.shape
    rank = low_columns // 3
    full[:, :columns] = sums_ref[...]
    for place in range(3):
        low = low_ref[:, place * rank : (place + 1) * rank]
        for far in (far_1, far_2, far_3):
            low = low + jnp.concatenate(
                [
                    far[at, row : row + 16, :].astype(F32)
                    for at, row, _ in low_places(far.shape, rows, place)
                ],
                axis=0,
            )
        full[:, columns + place * rank : columns + (place + 1) * rank] = low
    full[:, columns + low_columns :] = split_sum(
        jnp.sum(squares_ref[...], axis=1, keepdims=True), 128
    )
    share = rows // 4
    other = 1 - core
    send_ref[...] = jnp.concatenate(
        [
            full[aligned(other * share, share, 8), :],
            full[aligned((other + 2) * share, share, 8), :],
        ],
        axis=0,
    ).astype(BF16)
    keep_ref[:share, :] = full[aligned(core * share, share, 8), :]
    keep_ref[share:, :] = full[aligned((core + 2) * share, share, 8), :]


def second_send_body(keep_ref, arrived_ref, send_ref, kept_ref, full):
    chip = lax.axis_index("dp") // 2
    full[...] = keep_ref[...] + arrived_ref[...].astype(F32)
    full[:, -128:] = split_sum(jnp.sum(full[:, -128:], axis=1, keepdims=True), 128)
    share = full.shape[0] // 2
    send_ref[...] = full[aligned((1 - chip) * share, share, 8), :].astype(BF16)
    kept_ref[...] = full[aligned(chip * share, share, 8), :]


def attend_body(
    rows_dev,
    length_ref,
    trig_ref,
    kept_ref,
    arrived_ref,
    factors_0,
    factors_1,
    factors_2,
    factors_3,
    near,
    far_1,
    far_2,
    far_3,
    far_values,
    _,
    weight_ref,
    heads_ref,
    block_ref,
    low_query,
    low_narrow,
    turned,
    mixed,
    keys_all,
    values_all,
    sems,
):
    dp_index = lax.axis_index("dp")
    tensor_index = lax.axis_index("tensor")
    copies = fetch_copies(weight_ref, jnp.bitwise_xor(tensor_index, 2), 0, block_ref, sems)
    for copy in copies:
        copy.start()
    @pl.when(dp_index >= 0)
    def attended():
        rows = 2 * rows_dev
        span, head_dim = near.shape[1:]
        key_heads = keys_all.shape[0] // rows_dev
        query_columns = heads_ref.shape[1]
        heads = query_columns // head_dim
        group = heads // key_heads
        sources = lax.axis_size("tensor")
        rank = factors_0.shape[0]
        owners = lax.axis_size("dp")
        wide = query_columns // owners
        narrow = key_heads * head_dim // owners

        for place in range(rows_dev * key_heads):
            for mask, block in enumerate((near, far_1, far_2, far_3)):
                rows_here = slice(mask * span, (mask + 1) * span)
                keys_all[place, rows_here, :] = block[place]
                if mask == 3:
                    values_all[place, rows_here, :] = far_values[place]
                else:
                    values_all[place, rows_here, :] = block[rows_dev * key_heads + place]

        total = kept_ref[...] + arrived_ref[...].astype(F32)
        joint = query_columns + 2 * key_heads * head_dim
        squares = jnp.sum(total[:, -128:], axis=1, keepdims=True)
        scale = lax.rsqrt(squares / D + EPS)
        lows = [
            total[:, joint + place * rank : joint + (place + 1) * rank].astype(BF16)
            for place in range(3)
        ]
        for mask, factors in enumerate((factors_0, factors_1, factors_2, factors_3)):
            owner = jnp.bitwise_xor(dp_index, mask)
            low_query[owner] = jnp.dot(lows[0], factors[:, :wide], preferred_element_type=F32)
            pair = factors[:, wide : wide + 2 * narrow]
            for place in range(2):
                low_narrow[place, owner] = lax.dot_general(
                    lows[place + 1], pair, (((1,), (1,)), ((), ())), preferred_element_type=F32
                )
        cosine = trig_ref[:rows, :]
        sine = trig_ref[rows:, :]

        def turn(vector):
            return vector * cosine + pltpu.roll(vector, head_dim // 2, 1) * sine

        def rounded(vector):
            return vector.astype(BF16).astype(F32)

        for head in range(heads):
            column = head * head_dim
            owner, inner = column // wide, column % wide
            vector = (
                total[:, column : column + head_dim]
                + ADAPTER_SCALE * low_query[owner, :, inner : inner + head_dim]
            )
            start = (head % group) * rows
            turned[head // group, start : start + rows, :] = turn(rounded(vector * scale))

        lane = lax.broadcasted_iota(jnp.int32, (rows, head_dim), 1)
        per_head = head_dim // narrow
        fresh = [[], []]
        for place in range(2):
            for head in range(key_heads):
                low = jnp.zeros((rows, head_dim), F32)
                for part in range(per_head):
                    piece = low_narrow[place, head * per_head + part]
                    shift = (part * narrow - place * narrow) % (2 * narrow)
                    if shift:
                        piece = pltpu.roll(piece, shift, 1)
                    low = jnp.where(lane // narrow == part, piece, low)
                column = query_columns + place * key_heads * head_dim + head * head_dim
                vector = rounded(
                    (total[:, column : column + head_dim] + ADAPTER_SCALE * low) * scale
                )
                fresh[place].append(turn(vector) if place == 0 else vector)

        cached = sources * span
        width = keys_all.shape[1]
        column = lax.broadcasted_iota(jnp.int32, (1, width), 1)
        position = jnp.where(column == cached, -1, 1 << 30)
        for mask in range(sources):
            base = jnp.bitwise_xor(tensor_index, mask) * span
            inside = (column >= mask * span) & (column < (mask + 1) * span)
            position = jnp.where(inside, column - mask * span + base, position)
        step = lax.broadcasted_iota(jnp.int32, (2 * group, width), 0) % 2
        second = (step == 1) & (
            lax.broadcasted_iota(jnp.int32, (2 * group, width), 1) == cached + 1
        )
        score_scale = 1.0 / math.sqrt(head_dim)
        for row in range(rows_dev):
            valid = (position < length_ref[row : row + 1, :1]) | second
            for head in range(key_heads):
                place = row * key_heads + head
                for joined, parts in ((keys_all, fresh[0]), (values_all, fresh[1])):
                    joined[place, cached:, :] = jnp.concatenate(
                        [
                            parts[head][row : row + 1],
                            parts[head][rows_dev + row : rows_dev + row + 1],
                            jnp.zeros((width - cached - 2, head_dim), F32),
                        ],
                        axis=0,
                    ).astype(BF16)
                query = turned[head, pl.ds(row, 2 * group, stride=rows_dev), :].astype(BF16)
                scores = (
                    lax.dot_general(
                        query,
                        keys_all[place],
                        (((1,), (1,)), ((), ())),
                        preferred_element_type=F32,
                    )
                    * score_scale
                )
                scores = jnp.where(valid, scores, MASKED_FILLER)
                highest = jnp.max(scores, axis=1, keepdims=True)
                weights = jnp.where(valid, jnp.exp(scores - highest), 0.0)
                totals = jnp.sum(weights, axis=1, keepdims=True)
                weighted = jnp.dot(
                    weights.astype(BF16), values_all[place], preferred_element_type=F32
                )
                mixed[head, pl.ds(row, 2 * group, stride=rows_dev), :] = weighted / totals
        for head in range(heads):
            start = (head % group) * rows
            heads_ref[:, head * head_dim : (head + 1) * head_dim] = mixed[
                head // group, start : start + rows, :
            ].astype(BF16)

    for copy in copies:
        copy.wait()


def fetch_copies(weight_ref, target, first, block_ref, sems):
    depth, part = block_ref.shape
    pieces = sems.shape[0]
    rows = depth // pieces
    return [
        pltpu.make_async_copy(
            weight_ref.at[
                pl.ds(first + piece * rows, rows), aligned(target * part, part, 128)
            ],
            block_ref.at[pl.ds(piece * rows, rows)],
            sems.at[piece],
        )
        for piece in range(pieces)
    ]


def fetch_body(pieces, weight_ref, _, *blocks_and_sems):
    *blocks, sems = blocks_and_sems
    copies = []
    for place, ((mask, first), block_ref) in enumerate(zip(pieces, blocks)):
        target = jnp.bitwise_xor(lax.axis_index("tensor"), mask)
        copies += fetch_copies(weight_ref, target, first, block_ref, sems.at[place])
    for copy in copies:
        copy.start()
    for copy in copies:
        copy.wait()


def product(rows_ref, *blocks):
    width = math.gcd(blocks[0].shape[1], 512)
    results = []
    for start in range(0, blocks[0].shape[1], width):
        first, result = 0, None
        for block in blocks:
            depth = block.shape[0]
            term = jnp.dot(
                rows_ref[:, first : first + depth],
                block[:, start : start + width],
                preferred_element_type=F32,
            )
            result = term if result is None else result + term
            first += depth
        results.append(result)
    return jnp.concatenate(results, axis=1)


def far_output_body(
    mask,
    first,
    heads_0,
    heads_1,
    heads_2,
    heads_3,
    factors_0,
    factors_1,
    factors_2,
    factors_3,
    block_ref,
    _,
    weight_ref,
    send_ref,
    low_ref,
    all_rows,
    fetched_ref,
    wide_rows,
    sems,
):
    dp_index = lax.axis_index("dp")
    target = jnp.bitwise_xor(lax.axis_index("tensor"), mask)
    copies = fetch_copies(weight_ref, target, first, fetched_ref, sems)
    for copy in copies:
        copy.start()
    @pl.when(dp_index >= 0)
    def multiplied():
        share = heads_0.shape[0]
        for distance, part in enumerate((heads_0, heads_1, heads_2, heads_3)):
            owner = jnp.bitwise_xor(dp_index, distance)
            wide_rows[aligned(owner * share, share, 8), :] = part[...].astype(F32)
        all_rows[...] = wide_rows[...].astype(BF16)
        rank = factors_0.shape[0]
        block = all_rows.shape[1] // lax.axis_size("dp")
        pieces = block // rank
        base = factors_0.shape[1] - pieces * rank
        low = jnp.zeros((all_rows.shape[0], rank), F32)
        for distance, factors in enumerate((factors_0, factors_1, factors_2, factors_3)):
            owner = jnp.bitwise_xor(dp_index, distance)
            for piece in range(pieces):
                low = low + jnp.dot(
                    all_rows[:, aligned(owner * block + piece * rank, rank, 128)],
                    factors[:, base + piece * rank : base + (piece + 1) * rank],
                    preferred_element_type=F32,
                )
        low_ref[...] = low
        part = block_ref.shape[1]
        send_ref[:, :part] = product(all_rows, block_ref).astype(BF16)
        send_ref[:, part:] = low.astype(BF16)

    for copy in copies:
        copy.wait()


def next_output_body(all_rows, low_ref, *blocks_and_result):
    *blocks, result_ref = blocks_and_result
    part = blocks[0].shape[1]
    result_ref[:, :part] = product(all_rows, *blocks).astype(result_ref.dtype)
    result_ref[:, part:] = low_ref[...].astype(result_ref.dtype)


def own_output_body(all_rows, low_ref, weight_ref, result_ref, held, sems):
    copies = fetch_copies(weight_ref, lax.axis_index("tensor"), 0, held, sems)
    for copy in copies:
        copy.start()
    part = held.shape[1]
    rows = held.shape[0] // len(copies)
    result_ref[:, part:] = low_ref[...]
    for piece, copy in enumerate(copies):
        copy.wait()
        here = slice(piece * rows, (piece + 1) * rows)
        term = jnp.dot(all_rows[:, here], held[here, :], preferred_element_type=F32)
        if piece == 0:
            result_ref[:, :part] = term
        else:
            result_ref[:, :part] += term


def add_far_body(keep_ref, far, sum_ref):
    sum_ref[...] = keep_ref[...] + far[...].astype(F32)


def finish_body(rows_dev, sum_ref, far_1, b_out_ref, part_ref):
    total = sum_ref[...] + far_1[...].astype(F32)
    part = b_out_ref.shape[1]
    low = total[:, part:].astype(BF16)
    result = total[:, :part] + ADAPTER_SCALE * jnp.dot(
        low, b_out_ref[...], preferred_element_type=F32
    )
    pieces = []
    for step in range(2):
        for owner in range(result.shape[0] // (2 * rows_dev)):
            start = (2 * owner + step) * rows_dev
            pieces.append(result[start : start + rows_dev])
    part_ref[...] = jnp.concatenate(pieces, axis=0).astype(BF16)


def place_body(part_0, part_1, part_2, part_3, first_ref, second_ref, sems):
    tensor_index = lax.axis_index("tensor")
    rows = first_ref.shape[0]
    copies = []
    for mask, part in enumerate((part_0, part_1, part_2, part_3)):
        width = part.shape[1]
        columns = aligned(jnp.bitwise_xor(tensor_index, mask) * width, width, 128)
        for step, target in enumerate((first_ref, second_ref)):
            copies.append(
                pltpu.make_async_copy(
                    part.at[pl.ds(step * rows, rows)],
                    target.at[:, columns],
                    sems.at[mask, step],
                )
            )
    for copy in copies:
        copy.start()
    for copy in copies:
        copy.wait()


def on_device_joined(
    hidden_first,
    hidden_second,
    norm_gain,
    query_weight,
    w_key,
    w_value,
    w_out,
    a_query,
    b_query,
    a_key,
    b_key,
    a_value,
    b_value,
    a_out,
    b_out,
    cache_keys,
    cache_values,
    lengths,
):
    shape = jax.ShapeDtypeStruct
    rows, width = hidden_first.shape
    rows_dev, all_key_heads, span, head_dim = cache_keys.shape
    n_tensor = lax.axis_size("tensor")
    key_heads = all_key_heads // n_tensor
    rank = a_query.shape[1]
    query_columns = query_weight.shape[1]
    key_columns = w_key.shape[1]
    joint = query_columns + 2 * key_columns
    both = 2 * rows
    share = 2 * rows_dev
    low_columns = 3 * rank
    blocks = 2 * rows_dev * key_heads
    low_blocks = -(-3 * both // span)
    pack_columns = b_query.shape[1] + rank + a_out.shape[0]

    scaled, squares, low, near, far_1, far_2, far_3, far_values, factors = kernel_call(
        functools.partial(prepare_body, rows_dev),
        (
            shape((both, width), BF16),
            shape((both, 128), F32),
            shape((both, low_columns), F32),
            shape((blocks, span, head_dim), BF16),
            shape((blocks + low_blocks, span, head_dim), BF16),
            shape((blocks + low_blocks, span, head_dim), BF16),
            shape((blocks // 2 + low_blocks, span, head_dim), BF16),
            shape((blocks // 2, span, head_dim), BF16),
            shape((rank, pack_columns), BF16),
        ),
        [hbm_spec()] * 12,
        [
            pltpu.VMEM((2, rows, width), BF16),
            pltpu.VMEM((width // 128, 128), BF16),
            pltpu.VMEM((3,) + a_query.shape, BF16),
            pltpu.SemaphoreType.DMA((3,)),
        ],
        moved=12e6,
    )(
        *in_hbm(
            hidden_first,
            hidden_second,
            norm_gain.reshape(width // 128, 128),
            a_query,
            a_key,
            a_value,
            cache_keys,
            cache_values,
            b_query,
            b_key.T,
            b_value.T,
            a_out,
        )
    )
    far = [swapped(part, "tensor", mask) for mask, part in ((1, far_1), (2, far_2), (3, far_3))]
    factors_x = swapped(factors, "dp", 2)
    factors_core = swapped(factors, "dp", 1)

    depth = math.gcd(width, 256)
    sums, trig, length = kernel_call(
        functools.partial(project_body, rows_dev),
        (
            shape((both, joint), F32),
            shape((2 * share, head_dim), F32),
            shape((share, head_dim), jnp.int32),
        ),
        [hbm_spec(), vmem_spec(), hbm_spec(), hbm_spec(), hbm_spec()],
        [
            pltpu.VMEM((4, depth, query_columns), BF16),
            pltpu.VMEM((width, key_columns), BF16),
            pltpu.VMEM((width, key_columns), BF16),
            pltpu.SMEM((rows_dev,), jnp.int32),
            pltpu.SemaphoreType.DMA((4,)),
            pltpu.SemaphoreType.DMA((3,)),
        ],
        moved=2 * width * joint,
        mib=16,
    )(*in_hbm(lengths), scaled, *in_hbm(query_weight, w_key, w_value))
    heads_here = query_columns // head_dim
    out_columns = w_out.shape[1]
    part = out_columns // n_tensor
    eighth = w_out.shape[0] // 8

    def weight_block(eighths):
        return pltpu.VMEM((eighths * eighth, part), BF16)

    (w_out,) = in_hbm(w_out)
    fetch_sems = pltpu.SemaphoreType.DMA((4,))

    def fetched(after, *pieces):
        return kernel_call(
            functools.partial(
                fetch_body, [(mask, first * eighth) for mask, first, _ in pieces]
            ),
            tuple(weight_block(eighths) for _, _, eighths in pieces),
            [hbm_spec(), any_spec()],
            [pltpu.SemaphoreType.DMA((len(pieces), 4))],
            mib=4,
            moved=2 * sum(eighths for _, _, eighths in pieces) * eighth * part,
        )(w_out, after)

    extended = joint + low_columns + 128
    send, keep = kernel_call(
        first_send_body,
        (shape((rows, extended), BF16), shape((rows, extended), F32)),
        [vmem_spec()] * 6,
        [pltpu.VMEM((both, extended), F32)],
    )(sums, low, squares, *far)
    factors_x, far_values, send = lax.optimization_barrier((factors_x, far_values, send))
    far_values = swapped(far_values, "tensor", 3)
    factors_both = swapped(factors_x, "dp", 1)
    all_factors = (factors, factors_core, factors_x, factors_both)
    arrived = swapped(send, "dp", 1)
    send, kept = kernel_call(
        second_send_body,
        (shape((share, extended), BF16), shape((share, extended), F32)),
        [vmem_spec()] * 2,
        [pltpu.VMEM((rows, extended), F32)],
    )(keep, arrived)
    arrived = swapped(send, "dp", 2)
    (block_3,) = fetched(send, (3, 0, 8))
    group = heads_here // key_heads
    positions = n_tensor * span + 16
    owners = lax.axis_size("dp")
    heads, block_2 = kernel_call(
        functools.partial(attend_body, rows_dev),
        (shape((share, query_columns), BF16), weight_block(6)),
        [vmem_spec()] * 13 + [any_spec(), hbm_spec()],
        [
            pltpu.VMEM((owners, share, query_columns // owners), F32),
            pltpu.VMEM((2, owners, share, 2 * key_columns // owners), F32),
            pltpu.VMEM((key_heads, group * share, head_dim), F32),
            pltpu.VMEM((key_heads, group * share, head_dim), F32),
            pltpu.VMEM((rows_dev * key_heads, positions, head_dim), BF16),
            pltpu.VMEM((rows_dev * key_heads, positions, head_dim), BF16),
            fetch_sems,
        ],
        moved=10e6,
    )(length, trig, kept, arrived, *all_factors, near, *far, far_values, block_3, w_out)

    heads_x = swapped(heads, "dp", 2)
    heads_core = swapped(heads, "dp", 1)
    last_2, block_1 = fetched(heads, (2, 6, 2), (1, 0, 4))
    heads_x, _ = lax.optimization_barrier((heads_x, block_1))
    heads_both = swapped(heads_x, "dp", 1)
    message = shape((both, part + rank), BF16)
    summed = shape((both, part + rank), F32)
    send_3, low, all_rows, last_1 = kernel_call(
        functools.partial(far_output_body, 1, 4 * eighth),
        (
            message,
            shape((both, rank), F32),
            shape((both, w_out.shape[0]), BF16),
            weight_block(4),
        ),
        [vmem_spec()] * 9 + [any_spec(), hbm_spec()],
        [pltpu.VMEM((both, w_out.shape[0]), F32), fetch_sems],
        mib=8,
        moved=10e6,
    )(heads, heads_core, heads_x, heads_both, *all_factors, block_3, block_1, w_out)
    far_3 = swapped(send_3, "tensor", 3)

    def next_output(*weights):
        return kernel_call(
            next_output_body,
            (message,),
            [vmem_spec()] * (2 + len(weights)),
            mib=8,
            moved=40e6,
        )(all_rows, low, *weights)[0]

    def added(total, far_part, moved):
        return kernel_call(add_far_body, (summed,), [vmem_spec()] * 2, mib=8, moved=moved)(
            total, far_part
        )[0]

    far_2 = swapped(next_output(block_2, last_2), "tensor", 2)
    far_1 = swapped(next_output(block_1, last_1), "tensor", 1)
    (total,) = kernel_call(
        own_output_body,
        (summed,),
        [vmem_spec(), vmem_spec(), hbm_spec()],
        [weight_block(8), pltpu.SemaphoreType.DMA((8,))],
        mib=12,
        moved=40e6,
    )(all_rows, low, w_out)
    total = added(added(total, far_3, 40e6), far_2, 40e6)
    (done,) = kernel_call(
        functools.partial(finish_body, rows_dev),
        (shape((both, part), BF16),),
        [vmem_spec()] * 3,
        mib=8,
    )(total, far_1, b_out)
    parts = [done] + [swapped(done, "tensor", mask) for mask in (1, 2, 3)]
    return kernel_call(
        place_body,
        (shape((rows, out_columns), BF16), shape((rows, out_columns), BF16)),
        [vmem_spec()] * 4,
        [pltpu.SemaphoreType.DMA((4, 2))],
        out_specs=(hbm_spec(), hbm_spec()),
    )(*parts)


def takes_joined(mesh):
    return mesh.shape["dp"] == 4 and mesh.shape["tensor"] == 4


def solution(mesh):
    in_specs = (
        P("groups", "dp"),
        P("groups", "dp"),
        P("dp"),
        P("dp", "tensor"),
        P("dp", "tensor"),
        P("dp", "tensor"),
        P("tensor", "dp"),
        P(("dp", "tensor"), None),
        P(None, ("tensor", "dp")),
        P(("dp", "tensor"), None),
        P(None, ("tensor", "dp")),
        P(("dp", "tensor"), None),
        P(None, ("tensor", "dp")),
        P(("tensor", "dp"), None),
        P(None, ("dp", "tensor")),
        P(("groups", "dp"), None, "tensor", None),
        P(("groups", "dp"), None, "tensor", None),
        P(("groups", "dp")),
    )
    out_specs = (P("groups", "dp"), P("groups", "dp"))
    return jax.shard_map(
        on_device_joined if takes_joined(mesh) else on_device,
        mesh=mesh,
        in_specs=in_specs,
        out_specs=out_specs,
        check_vma=False,
    )
```

```python
import functools
import math

import jax
import jax.numpy as jnp
import numpy as np
from jax import lax
from jax.experimental import pallas as pl
from jax.experimental.pallas import tpu as pltpu
from jax.sharding import PartitionSpec as P

D = 16384


ADAPTER_SCALE = 2.0
ROPE_BASE = 500000.0
EPS = 1e-05
MASKED_FILLER = -1e30
BF16 = jnp.bfloat16
F32 = jnp.float32


def joined_2(part, axis, combine):
    gathered = jax.tree.map(lambda a: lax.all_gather(a, axis), part)

    def take(source):
        return jax.tree.map(lambda a: lax.dynamic_index_in_dim(a, source, 0, False), gathered)

    return lax.fori_loop(
        1, lax.axis_size(axis), lambda source, state: combine(state, take(source)), take(0)
    )


def merge_weight(frozen_weight, factor_in, factor_out):
    adapter_update = jnp.dot(factor_in, factor_out, preferred_element_type=jnp.float32)
    return (frozen_weight.astype(jnp.float32) + ADAPTER_SCALE * adapter_update).astype(jnp.bfloat16)


def rotary(vectors, positions_now):
    half_dim = vectors.shape[-1] // 2
    frequency = ROPE_BASE ** (-jnp.arange(half_dim, dtype=jnp.float32) / half_dim)
    angles = positions_now.astype(jnp.float32)[:, None] * frequency[None, :]
    cosine = jnp.cos(angles)[:, None, :]
    sine_part = jnp.sin(angles)[:, None, :]
    lower = vectors[..., :half_dim]
    upper = vectors[..., half_dim:]
    return jnp.concatenate(
        [lower * cosine - upper * sine_part, upper * cosine + lower * sine_part], axis=-1
    )


def combine_partial(earlier, later):
    highest = jnp.maximum(earlier[0], later[0])
    weight_a = jnp.exp(earlier[0] - highest)
    weight_b = jnp.exp(later[0] - highest)
    return (
        highest,
        earlier[1] * weight_a + later[1] * weight_b,
        earlier[2] * weight_a[..., None] + later[2] * weight_b[..., None],
    )


def on_device(
    hidden_first,
    hidden_second,
    norm_gain,
    query_weight,
    w_key,
    w_value,
    w_out,
    a_query,
    b_query,
    a_key,
    b_key,
    a_value,
    b_value,
    a_out,
    b_out,
    cache_keys,
    cache_values,
    lengths,
):
    tensor_parts = (
        lax.all_gather(a_query, "tensor", axis=0, tiled=True),
        lax.all_gather(a_key, "tensor", axis=0, tiled=True),
        lax.all_gather(a_value, "tensor", axis=0, tiled=True),
        lax.all_gather(b_out, "tensor", axis=1, tiled=True),
    )
    data_parts = (
        lax.all_gather(b_query, "dp", axis=1, tiled=True),
        lax.all_gather(b_key, "dp", axis=1, tiled=True),
        lax.all_gather(b_value, "dp", axis=1, tiled=True),
        lax.all_gather(a_out, "dp", axis=0, tiled=True),
    )
    merged_qkv = jnp.concatenate(
        [
            merge_weight(query_weight, tensor_parts[0], data_parts[0]),
            merge_weight(w_key, tensor_parts[1], data_parts[1]),
            merge_weight(w_value, tensor_parts[2], data_parts[2]),
        ],
        axis=1,
    )
    merged_output = merge_weight(w_out, data_parts[3], tensor_parts[3])
    n_tensor = lax.axis_size("tensor")
    tensor_index = lax.axis_index("tensor")
    rows_dev, key_value_heads, cache_span, head_dim = cache_keys.shape
    query_cols = query_weight.shape[1]
    key_cols = w_key.shape[1]
    joint_cols = query_cols + 2 * key_cols
    heads_here = query_cols // head_dim
    all_heads = heads_here * n_tensor
    group_size = all_heads // key_value_heads
    score_scale = 1.0 / math.sqrt(head_dim)
    cache_positions = tensor_index * cache_span + jnp.arange(cache_span, dtype=jnp.int32)
    cache_valid = cache_positions[None, :] < lengths[:, None]
    first_owner = tensor_index == 0
    fresh_keys = []
    fresh_values = []
    results = []
    for step_index, hidden in enumerate((hidden_first, hidden_second)):
        values_f = hidden.astype(jnp.float32)
        squares = lax.psum(jnp.sum(values_f * values_f, axis=1), "dp")
        normed = (
            values_f * lax.rsqrt(squares / D + EPS)[:, None] * norm_gain.astype(jnp.float32)
        ).astype(jnp.bfloat16)
        projected = lax.psum_scatter(
            jnp.dot(normed, merged_qkv, preferred_element_type=jnp.float32),
            "dp",
            scatter_dimension=0,
            tiled=True,
        ).astype(jnp.bfloat16)
        joined = lax.all_gather(projected, "tensor", axis=1, tiled=True).reshape(
            rows_dev, n_tensor, joint_cols
        )
        queries = joined[:, :, :query_cols].reshape(rows_dev, all_heads, head_dim)
        key_now = joined[:, :, query_cols : query_cols + key_cols].reshape(
            rows_dev, key_value_heads, head_dim
        )
        value_now = joined[:, :, query_cols + key_cols :].reshape(
            rows_dev, key_value_heads, head_dim
        )
        positions_now = lengths + step_index
        queries = rotary(queries.astype(jnp.float32), positions_now).astype(jnp.bfloat16)
        queries = queries.reshape(rows_dev, key_value_heads, group_size, head_dim)
        fresh_keys.append(rotary(key_now.astype(jnp.float32), positions_now).astype(jnp.bfloat16))
        fresh_values.append(value_now)
        cache_scores = (
            jnp.einsum("rkgd,rksd->rkgs", queries, cache_keys, preferred_element_type=jnp.float32)
            * score_scale
        )
        cache_scores = jnp.where(cache_valid[:, None, None, :], cache_scores, MASKED_FILLER)
        new_scores = (
            jnp.einsum(
                "rkgd,rknd->rkgn",
                queries,
                jnp.stack(fresh_keys, axis=2),
                preferred_element_type=jnp.float32,
            )
            * score_scale
        )
        new_scores = jnp.where(first_owner, new_scores, MASKED_FILLER)
        highest = jnp.maximum(jnp.max(cache_scores, axis=-1), jnp.max(new_scores, axis=-1))
        cache_weights = jnp.where(
            cache_valid[:, None, None, :], jnp.exp(cache_scores - highest[..., None]), 0.0
        )
        new_weights = jnp.where(first_owner, jnp.exp(new_scores - highest[..., None]), 0.0)
        totals = jnp.sum(cache_weights, axis=-1) + jnp.sum(new_weights, axis=-1)
        weighted = jnp.einsum(
            "rkgs,rksd->rkgd", cache_weights, cache_values, preferred_element_type=jnp.float32
        )
        weighted = weighted + jnp.einsum(
            "rkgn,rknd->rkgd",
            new_weights,
            jnp.stack(fresh_values, axis=2),
            preferred_element_type=jnp.float32,
        )
        highest = highest.reshape(rows_dev, all_heads)
        totals = totals.reshape(rows_dev, all_heads)
        weighted = weighted.reshape(rows_dev, all_heads, head_dim)
        high_all, total_all, weighted_all = joined_2(
            (highest, totals, weighted), "tensor", combine_partial
        )
        normalized = weighted_all / total_all[..., None]
        own_heads = lax.dynamic_slice_in_dim(normalized, tensor_index * heads_here, heads_here, 1)
        heads = own_heads.reshape(rows_dev, query_cols).astype(jnp.bfloat16)
        out_terms = jnp.dot(
            lax.all_gather(heads, "dp", axis=0, tiled=True),
            merged_output,
            preferred_element_type=jnp.float32,
        )
        attn_out = lax.psum(out_terms, "tensor").astype(jnp.bfloat16)
        results.append(attn_out)
    return (results[0], results[1])

def swapped(array, axis, mask):
    size = lax.axis_size(axis)
    return lax.ppermute(array, axis, [(k, k ^ mask) for k in range(size)])


def vmem_spec():
    return pl.BlockSpec(memory_space=pltpu.VMEM)


def any_spec():
    return pl.BlockSpec(memory_space=pl.ANY)


def hbm_spec():
    return pl.BlockSpec(memory_space=pltpu.HBM)


def in_hbm(*arrays):
    return [pltpu.with_memory_space_constraint(array, pltpu.HBM) for array in arrays]


def cost(moved):
    return pl.CostEstimate(flops=0, bytes_accessed=int(moved), transcendentals=0)


def kernel_call(body, outs, in_specs, scratch=(), mib=12, out_specs=None, moved=0):
    return pl.pallas_call(
        body,
        out_shape=outs,
        in_specs=in_specs,
        out_specs=out_specs or tuple(vmem_spec() for _ in outs),
        scratch_shapes=list(scratch),
        cost_estimate=cost(moved),
        compiler_params=pltpu.CompilerParams(vmem_limit_bytes=mib << 20),
    )


def aligned(start, size, unit):
    return pl.ds(pl.multiple_of(start, unit), size)


def split_sum(total, width):
    high = total.astype(BF16).astype(F32)
    rest = total - high
    middle = rest.astype(BF16).astype(F32)
    low = rest - middle
    lane = lax.broadcasted_iota(jnp.int32, (total.shape[0], width), 1)
    return jnp.where(
        lane == 0, high, jnp.where(lane == 1, middle, jnp.where(lane == 2, low, 0.0))
    )


def low_places(shape, rows, place):
    blocks, span, _ = shape
    first = blocks - -(-3 * rows // span)
    for part in range(0, rows, 16):
        flat = place * rows + part
        yield first + flat // span, flat % span, part


def prepare_body(
    rows_dev,
    first_ref,
    second_ref,
    gain_ref,
    a_query_ref,
    a_key_ref,
    a_value_ref,
    keys_ref,
    values_ref,
    b_query_ref,
    b_key_ref,
    b_value_ref,
    a_out_ref,
    _,
    scaled_ref,
    squares_ref,
    low_ref,
    near,
    far_1,
    far_2,
    far_3,
    far_late,
    factors_ref,
    hidden,
    gain_held,
    a_held,
    sems,
):
    tensor_index = lax.axis_index("tensor")
    heads_here = keys_ref.shape[1] // lax.axis_size("tensor")
    rank = a_query_ref.shape[1]
    wide = b_query_ref.shape[1]
    narrow = b_key_ref.shape[0]

    def begun(group, pairs):
        copies = [pltpu.make_async_copy(*pair, sems.at[group]) for pair in pairs]
        for copy in copies:
            copy.start()
        return copies

    inputs = begun(
        0, [(first_ref, hidden.at[0]), (second_ref, hidden.at[1]), (gain_ref, gain_held)]
    )
    inputs += begun(
        1,
        [(ref, a_held.at[place]) for place, ref in enumerate((a_query_ref, a_key_ref, a_value_ref))],
    )
    moves = []
    for mask, far in enumerate((near, far_1, far_2, far_3)):
        head = jnp.bitwise_xor(tensor_index, mask) * heads_here
        for kind, cache in enumerate((keys_ref, values_ref)):
            for row in range(rows_dev):
                late = mask == 3 and (kind == 1 or row == rows_dev - 1)
                if late:
                    start = (row if kind == 1 else rows_dev) * heads_here
                else:
                    start = (kind * rows_dev + row) * heads_here
                target = far_late if late else far
                moves.append(
                    (cache.at[row, pl.ds(head, heads_here)], target.at[pl.ds(start, heads_here)])
                )
    moves.append((b_query_ref, factors_ref.at[:, pl.ds(0, wide)]))
    for place, ref in enumerate((b_key_ref, b_value_ref)):
        moves.append((ref, factors_ref.at[pl.ds(place * narrow, narrow), pl.ds(wide, rank)]))
    for piece in range(a_out_ref.shape[0] // rank):
        moves.append(
            (
                a_out_ref.at[pl.ds(piece * rank, rank)],
                factors_ref.at[:, pl.ds(wide + (piece + 1) * rank, rank)],
            )
        )
    moves = begun(2, moves)
    @pl.when(tensor_index >= 0)
    def scaled():
        for copy in inputs[:3]:
            copy.wait()
        rows, width = first_ref.shape
        pieces = []
        sums = [jnp.zeros((rows, 128), F32), jnp.zeros((rows, 128), F32)]

        def by_owner(pair):
            ordered = []
            for owner in range(rows // rows_dev):
                for part in pair:
                    ordered.append(part[owner * rows_dev : (owner + 1) * rows_dev])
            return jnp.concatenate(ordered, axis=0)

        for piece in range(width // 128):
            columns = slice(piece * 128, (piece + 1) * 128)
            steps = [hidden[step, :, columns].astype(F32) for step in range(2)]
            sums = [total + step * step for total, step in zip(sums, steps)]
            gain = gain_held[piece : piece + 1, :].astype(F32)
            scaled_ref[:, columns] = by_owner([step * gain for step in steps]).astype(BF16)
        squares_ref[...] = by_owner(sums)
        for copy in inputs[3:]:
            copy.wait()
        depth = a_query_ref.shape[0]
        own = scaled_ref[:, aligned(tensor_index * depth, depth, 128)]
        low_rows = scaled_ref.shape[0]
        for place in range(3):
            low = jnp.dot(own, a_held[place], preferred_element_type=F32)
            low_ref[:, place * rank : (place + 1) * rank] = low
            for far in (far_1, far_2, far_3):
                for at, row, part in low_places(far.shape, low_rows, place):
                    far[at, row : row + 16, :] = low[part : part + 16].astype(BF16)

    for copy in moves:
        copy.wait()


def project_body(
    rows_dev,
    lengths_ref,
    scaled_ref,
    query_ref,
    key_ref,
    value_ref,
    sums_ref,
    trig_ref,
    length_ref,
    ring,
    lengths_held,
    ring_sem,
    held_sem,
):
    slots, depth, columns = ring.shape
    chunks = query_ref.shape[0] // depth

    def fetch(chunk):
        slot = chunk % slots
        return pltpu.make_async_copy(
            query_ref.at[pl.ds(chunk * depth, depth)], ring.at[slot], ring_sem.at[slot]
        )

    for chunk in range(min(slots, chunks)):
        fetch(chunk).start()
    lengths_copy = pltpu.make_async_copy(lengths_ref, lengths_held, held_sem.at[0])
    lengths_copy.start()
    lengths_copy.wait()
    shape = length_ref.shape
    half = shape[1] // 2
    row = lax.broadcasted_iota(jnp.int32, shape, 0)
    lane = lax.broadcasted_iota(jnp.int32, shape, 1)
    length = jnp.zeros(shape, jnp.int32)
    for place in range(rows_dev):
        length = length + jnp.where(row % rows_dev == place, lengths_held[place], 0)
    length_ref[...] = length
    exponent = (lane % half).astype(F32) / half
    frequency = jnp.exp(exponent * (-math.log(ROPE_BASE)))
    angles = (length + row // rows_dev).astype(F32) * frequency
    sine = jnp.sin(angles)
    trig_ref[: shape[0], :] = jnp.cos(angles)
    trig_ref[shape[0] :, :] = jnp.where(lane < half, -sine, sine)
    place = columns
    for held in (key_ref, value_ref):
        sums_ref[:, place : place + held.shape[1]] = jnp.dot(
            scaled_ref[...], held[...], preferred_element_type=F32
        )
        place += held.shape[1]
    for chunk in range(chunks):
        fetch(chunk).wait()
        term = jnp.dot(
            scaled_ref[:, chunk * depth : (chunk + 1) * depth],
            ring[chunk % slots],
            preferred_element_type=F32,
        )
        if chunk == 0:
            sums_ref[:, :columns] = term
        else:
            sums_ref[:, :columns] += term
        if chunk + slots < chunks:
            fetch(chunk + slots).start()


def first_send_body(sums_ref, low_ref, squares_ref, far_1, far_2, far_3, send_ref, keep_ref, full):
    core = lax.rem(lax.axis_index("dp"), 2)
    columns = sums_ref.shape[1]
    rows, low_columns = low_ref.shape
    rank = low_columns // 3
    full[:, :columns] = sums_ref[...]
    for place in range(3):
        low = low_ref[:, place * rank : (place + 1) * rank]
        for far in (far_1, far_2, far_3):
            low = low + jnp.concatenate(
                [
                    far[at, row : row + 16, :].astype(F32)
                    for at, row, _ in low_places(far.shape, rows, place)
                ],
                axis=0,
            )
        full[:, columns + place * rank : columns + (place + 1) * rank] = low
    full[:, columns + low_columns :] = split_sum(
        jnp.sum(squares_ref[...], axis=1, keepdims=True), 128
    )
    share = rows // 4
    other = 1 - core
    send_ref[...] = jnp.concatenate(
        [
            full[aligned(other * share, share, 8), :],
            full[aligned((other + 2) * share, share, 8), :],
        ],
        axis=0,
    ).astype(BF16)
    keep_ref[:share, :] = full[aligned(core * share, share, 8), :]
    keep_ref[share:, :] = full[aligned((core + 2) * share, share, 8), :]


def second_send_body(keep_ref, arrived_ref, send_ref, kept_ref, full):
    chip = lax.axis_index("dp") // 2
    full[...] = keep_ref[...] + arrived_ref[...].astype(F32)
    full[:, -128:] = split_sum(jnp.sum(full[:, -128:], axis=1, keepdims=True), 128)
    share = full.shape[0] // 2
    send_ref[...] = full[aligned((1 - chip) * share, share, 8), :].astype(BF16)
    kept_ref[...] = full[aligned(chip * share, share, 8), :]


def attend_body(
    rows_dev,
    length_ref,
    trig_ref,
    kept_ref,
    arrived_ref,
    factors_0,
    factors_1,
    factors_2,
    factors_3,
    near,
    far_1,
    far_2,
    far_3,
    far_late,
    _,
    weight_ref,
    heads_ref,
    block_ref,
    low_query,
    low_narrow,
    turned,
    mixed,
    keys_all,
    values_all,
    sems,
):
    dp_index = lax.axis_index("dp")
    tensor_index = lax.axis_index("tensor")
    copies = fetch_copies(weight_ref, jnp.bitwise_xor(tensor_index, 2), 0, block_ref, sems)
    for copy in copies:
        copy.start()
    @pl.when(dp_index >= 0)
    def attended():
        rows = 2 * rows_dev
        span, head_dim = near.shape[1:]
        key_heads = keys_all.shape[0] // rows_dev
        query_columns = heads_ref.shape[1]
        heads = query_columns // head_dim
        group = heads // key_heads
        sources = lax.axis_size("tensor")
        rank = factors_0.shape[0]
        owners = lax.axis_size("dp")
        wide = query_columns // owners
        narrow = key_heads * head_dim // owners

        for place in range(rows_dev * key_heads):
            last = place - (rows_dev - 1) * key_heads
            for mask, block in enumerate((near, far_1, far_2, far_3)):
                rows_here = slice(mask * span, (mask + 1) * span)
                key_block, value_block = block, block
                key_place, value_place = place, rows_dev * key_heads + place
                if mask == 3:
                    value_block, value_place = far_late, place
                    if last >= 0:
                        key_block, key_place = far_late, rows_dev * key_heads + last
                keys_all[place, rows_here, :] = key_block[key_place]
                values_all[place, rows_here, :] = value_block[value_place]

        total = kept_ref[...] + arrived_ref[...].astype(F32)
        joint = query_columns + 2 * key_heads * head_dim
        squares = jnp.sum(total[:, -128:], axis=1, keepdims=True)
        scale = lax.rsqrt(squares / D + EPS)
        lows = [
            total[:, joint + place * rank : joint + (place + 1) * rank].astype(BF16)
            for place in range(3)
        ]
        for mask, factors in enumerate((factors_0, factors_1, factors_2, factors_3)):
            owner = jnp.bitwise_xor(dp_index, mask)
            low_query[owner] = jnp.dot(lows[0], factors[:, :wide], preferred_element_type=F32)
            pair = factors[:, wide : wide + 2 * narrow]
            for place in range(2):
                low_narrow[place, owner] = lax.dot_general(
                    lows[place + 1], pair, (((1,), (1,)), ((), ())), preferred_element_type=F32
                )
        cosine = trig_ref[:rows, :]
        sine = trig_ref[rows:, :]

        def turn(vector):
            return vector * cosine + pltpu.roll(vector, head_dim // 2, 1) * sine

        def rounded(vector):
            return vector.astype(BF16).astype(F32)

        for head in range(heads):
            column = head * head_dim
            owner, inner = column // wide, column % wide
            vector = (
                total[:, column : column + head_dim]
                + ADAPTER_SCALE * low_query[owner, :, inner : inner + head_dim]
            )
            start = (head % group) * rows
            turned[head // group, start : start + rows, :] = turn(rounded(vector * scale))

        lane = lax.broadcasted_iota(jnp.int32, (rows, head_dim), 1)
        per_head = head_dim // narrow
        fresh = [[], []]
        for place in range(2):
            for head in range(key_heads):
                low = jnp.zeros((rows, head_dim), F32)
                for part in range(per_head):
                    piece = low_narrow[place, head * per_head + part]
                    shift = (part * narrow - place * narrow) % (2 * narrow)
                    if shift:
                        piece = pltpu.roll(piece, shift, 1)
                    low = jnp.where(lane // narrow == part, piece, low)
                column = query_columns + place * key_heads * head_dim + head * head_dim
                vector = rounded(
                    (total[:, column : column + head_dim] + ADAPTER_SCALE * low) * scale
                )
                fresh[place].append(turn(vector) if place == 0 else vector)

        cached = sources * span
        width = keys_all.shape[1]
        column = lax.broadcasted_iota(jnp.int32, (1, width), 1)
        position = jnp.where(column == cached, -1, 1 << 30)
        for mask in range(sources):
            base = jnp.bitwise_xor(tensor_index, mask) * span
            inside = (column >= mask * span) & (column < (mask + 1) * span)
            position = jnp.where(inside, column - mask * span + base, position)
        step = lax.broadcasted_iota(jnp.int32, (2 * group, width), 0) % 2
        second = (step == 1) & (
            lax.broadcasted_iota(jnp.int32, (2 * group, width), 1) == cached + 1
        )
        score_scale = 1.0 / math.sqrt(head_dim)
        for row in range(rows_dev):
            valid = (position < length_ref[row : row + 1, :1]) | second
            for head in range(key_heads):
                place = row * key_heads + head
                for joined, parts in ((keys_all, fresh[0]), (values_all, fresh[1])):
                    joined[place, cached:, :] = jnp.concatenate(
                        [
                            parts[head][row : row + 1],
                            parts[head][rows_dev + row : rows_dev + row + 1],
                            jnp.zeros((width - cached - 2, head_dim), F32),
                        ],
                        axis=0,
                    ).astype(BF16)
                query = turned[head, pl.ds(row, 2 * group, stride=rows_dev), :].astype(BF16)
                scores = (
                    lax.dot_general(
                        query,
                        keys_all[place],
                        (((1,), (1,)), ((), ())),
                        preferred_element_type=F32,
                    )
                    * score_scale
                )
                scores = jnp.where(valid, scores, MASKED_FILLER)
                highest = jnp.max(scores, axis=1, keepdims=True)
                weights = jnp.where(valid, jnp.exp(scores - highest), 0.0)
                totals = jnp.sum(weights, axis=1, keepdims=True)
                weighted = jnp.dot(
                    weights.astype(BF16), values_all[place], preferred_element_type=F32
                )
                mixed[head, pl.ds(row, 2 * group, stride=rows_dev), :] = weighted / totals
        for head in range(heads):
            start = (head % group) * rows
            heads_ref[:, head * head_dim : (head + 1) * head_dim] = mixed[
                head // group, start : start + rows, :
            ].astype(BF16)

    for copy in copies:
        copy.wait()


def fetch_copies(weight_ref, target, first, block_ref, sems):
    depth, part = block_ref.shape
    pieces = sems.shape[0]
    rows = depth // pieces
    return [
        pltpu.make_async_copy(
            weight_ref.at[
                pl.ds(first + piece * rows, rows), aligned(target * part, part, 128)
            ],
            block_ref.at[pl.ds(piece * rows, rows)],
            sems.at[piece],
        )
        for piece in range(pieces)
    ]


def fetch_body(pieces, weight_ref, _, *blocks_and_sems):
    *blocks, sems = blocks_and_sems
    copies = []
    for place, ((mask, first), block_ref) in enumerate(zip(pieces, blocks)):
        target = jnp.bitwise_xor(lax.axis_index("tensor"), mask)
        copies += fetch_copies(weight_ref, target, first, block_ref, sems.at[place])
    for copy in copies:
        copy.start()
    for copy in copies:
        copy.wait()


def product(rows_ref, *blocks):
    width = math.gcd(blocks[0].shape[1], 512)
    results = []
    for start in range(0, blocks[0].shape[1], width):
        first, result = 0, None
        for block in blocks:
            depth = block.shape[0]
            term = jnp.dot(
                rows_ref[:, first : first + depth],
                block[:, start : start + width],
                preferred_element_type=F32,
            )
            result = term if result is None else result + term
            first += depth
        results.append(result)
    return jnp.concatenate(results, axis=1)


def far_output_body(
    mask,
    first,
    heads_0,
    heads_1,
    heads_2,
    heads_3,
    factors_0,
    factors_1,
    factors_2,
    factors_3,
    block_ref,
    _,
    weight_ref,
    send_ref,
    low_ref,
    all_rows,
    fetched_ref,
    wide_rows,
    sems,
):
    dp_index = lax.axis_index("dp")
    target = jnp.bitwise_xor(lax.axis_index("tensor"), mask)
    copies = fetch_copies(weight_ref, target, first, fetched_ref, sems)
    for copy in copies:
        copy.start()
    @pl.when(dp_index >= 0)
    def multiplied():
        share = heads_0.shape[0]
        for distance, part in enumerate((heads_0, heads_1, heads_2, heads_3)):
            owner = jnp.bitwise_xor(dp_index, distance)
            wide_rows[aligned(owner * share, share, 8), :] = part[...].astype(F32)
        all_rows[...] = wide_rows[...].astype(BF16)
        rank = factors_0.shape[0]
        block = all_rows.shape[1] // lax.axis_size("dp")
        pieces = block // rank
        base = factors_0.shape[1] - pieces * rank
        low = jnp.zeros((all_rows.shape[0], rank), F32)
        for distance, factors in enumerate((factors_0, factors_1, factors_2, factors_3)):
            owner = jnp.bitwise_xor(dp_index, distance)
            for piece in range(pieces):
                low = low + jnp.dot(
                    all_rows[:, aligned(owner * block + piece * rank, rank, 128)],
                    factors[:, base + piece * rank : base + (piece + 1) * rank],
                    preferred_element_type=F32,
                )
        low_ref[...] = low
        part = block_ref.shape[1]
        send_ref[:, :part] = product(all_rows, block_ref).astype(BF16)
        send_ref[:, part:] = low.astype(BF16)

    for copy in copies:
        copy.wait()


def next_output_body(all_rows, low_ref, *blocks_and_result):
    *blocks, result_ref = blocks_and_result
    part = blocks[0].shape[1]
    result_ref[:, :part] = product(all_rows, *blocks).astype(result_ref.dtype)
    result_ref[:, part:] = low_ref[...].astype(result_ref.dtype)


def own_output_body(all_rows, low_ref, weight_ref, result_ref, held, sems):
    copies = fetch_copies(weight_ref, lax.axis_index("tensor"), 0, held, sems)
    for copy in copies:
        copy.start()
    part = held.shape[1]
    rows = held.shape[0] // len(copies)
    result_ref[:, part:] = low_ref[...]
    for piece, copy in enumerate(copies):
        copy.wait()
        here = slice(piece * rows, (piece + 1) * rows)
        term = jnp.dot(all_rows[:, here], held[here, :], preferred_element_type=F32)
        if piece == 0:
            result_ref[:, :part] = term
        else:
            result_ref[:, :part] += term


def add_far_body(keep_ref, far, sum_ref):
    sum_ref[...] = keep_ref[...] + far[...].astype(F32)


def finish_body(rows_dev, sum_ref, far_1, b_out_ref, part_ref):
    total = sum_ref[...] + far_1[...].astype(F32)
    part = b_out_ref.shape[1]
    low = total[:, part:].astype(BF16)
    result = total[:, :part] + ADAPTER_SCALE * jnp.dot(
        low, b_out_ref[...], preferred_element_type=F32
    )
    pieces = []
    for step in range(2):
        for owner in range(result.shape[0] // (2 * rows_dev)):
            start = (2 * owner + step) * rows_dev
            pieces.append(result[start : start + rows_dev])
    part_ref[...] = jnp.concatenate(pieces, axis=0).astype(BF16)


def place_body(part_0, part_1, part_2, part_3, first_ref, second_ref, sems):
    tensor_index = lax.axis_index("tensor")
    rows = first_ref.shape[0]
    copies = []
    for mask, part in enumerate((part_0, part_1, part_2, part_3)):
        width = part.shape[1]
        columns = aligned(jnp.bitwise_xor(tensor_index, mask) * width, width, 128)
        for step, target in enumerate((first_ref, second_ref)):
            copies.append(
                pltpu.make_async_copy(
                    part.at[pl.ds(step * rows, rows)],
                    target.at[:, columns],
                    sems.at[mask, step],
                )
            )
    for copy in copies:
        copy.start()
    for copy in copies:
        copy.wait()


def on_device_joined(
    hidden_first,
    hidden_second,
    norm_gain,
    query_weight,
    w_key,
    w_value,
    w_out,
    a_query,
    b_query,
    a_key,
    b_key,
    a_value,
    b_value,
    a_out,
    b_out,
    cache_keys,
    cache_values,
    lengths,
):
    shape = jax.ShapeDtypeStruct
    rows, width = hidden_first.shape
    rows_dev, all_key_heads, span, head_dim = cache_keys.shape
    n_tensor = lax.axis_size("tensor")
    key_heads = all_key_heads // n_tensor
    rank = a_query.shape[1]
    query_columns = query_weight.shape[1]
    key_columns = w_key.shape[1]
    joint = query_columns + 2 * key_columns
    both = 2 * rows
    share = 2 * rows_dev
    low_columns = 3 * rank
    blocks = 2 * rows_dev * key_heads
    low_blocks = -(-3 * both // span)
    pack_columns = b_query.shape[1] + rank + a_out.shape[0]

    scaled, squares, low, near, far_1, far_2, far_3, far_late, factors = kernel_call(
        functools.partial(prepare_body, rows_dev),
        (
            shape((both, width), BF16),
            shape((both, 128), F32),
            shape((both, low_columns), F32),
            shape((blocks, span, head_dim), BF16),
            shape((blocks + low_blocks, span, head_dim), BF16),
            shape((blocks + low_blocks, span, head_dim), BF16),
            shape((blocks // 2 - key_heads + low_blocks, span, head_dim), BF16),
            shape((blocks // 2 + key_heads, span, head_dim), BF16),
            shape((rank, pack_columns), BF16),
        ),
        [hbm_spec()] * 13,
        [
            pltpu.VMEM((2, rows, width), BF16),
            pltpu.VMEM((width // 128, 128), BF16),
            pltpu.VMEM((3,) + a_query.shape, BF16),
            pltpu.SemaphoreType.DMA((3,)),
        ],
        moved=60e6,
    )(
        *in_hbm(
            hidden_first,
            hidden_second,
            norm_gain.reshape(width // 128, 128),
            a_query,
            a_key,
            a_value,
            cache_keys,
            cache_values,
            b_query,
            b_key.T,
            b_value.T,
            a_out,
            w_out,
        )
    )
    far = [swapped(part, "tensor", mask) for mask, part in ((1, far_1), (2, far_2), (3, far_3))]
    factors_x = swapped(factors, "dp", 2)
    factors_core = swapped(factors, "dp", 1)

    depth = math.gcd(width, 256)
    sums, trig, length = kernel_call(
        functools.partial(project_body, rows_dev),
        (
            shape((both, joint), F32),
            shape((2 * share, head_dim), F32),
            shape((share, head_dim), jnp.int32),
        ),
        [hbm_spec(), vmem_spec(), hbm_spec(), vmem_spec(), vmem_spec()],
        [
            pltpu.VMEM((4, depth, query_columns), BF16),
            pltpu.SMEM((rows_dev,), jnp.int32),
            pltpu.SemaphoreType.DMA((4,)),
            pltpu.SemaphoreType.DMA((1,)),
        ],
        moved=2 * width * joint,
        mib=16,
    )(*in_hbm(lengths), scaled, *in_hbm(query_weight), w_key, w_value)
    heads_here = query_columns // head_dim
    out_columns = w_out.shape[1]
    part = out_columns // n_tensor
    eighth = w_out.shape[0] // 8

    def weight_block(eighths):
        return pltpu.VMEM((eighths * eighth, part), BF16)

    (w_out,) = in_hbm(w_out)
    fetch_sems = pltpu.SemaphoreType.DMA((4,))

    def fetched(after, *pieces):
        return kernel_call(
            functools.partial(
                fetch_body, [(mask, first * eighth) for mask, first, _ in pieces]
            ),
            tuple(weight_block(eighths) for _, _, eighths in pieces),
            [hbm_spec(), any_spec()],
            [pltpu.SemaphoreType.DMA((len(pieces), 4))],
            mib=4,
            moved=2 * sum(eighths for _, _, eighths in pieces) * eighth * part,
        )(w_out, after)

    extended = joint + low_columns + 128
    send, keep = kernel_call(
        first_send_body,
        (shape((rows, extended), BF16), shape((rows, extended), F32)),
        [vmem_spec()] * 6,
        [pltpu.VMEM((both, extended), F32)],
    )(sums, low, squares, *far)
    factors_x, far_late, send = lax.optimization_barrier((factors_x, far_late, send))
    far_late = swapped(far_late, "tensor", 3)
    factors_both = swapped(factors_x, "dp", 1)
    all_factors = (factors, factors_core, factors_x, factors_both)
    arrived = swapped(send, "dp", 1)
    send, kept = kernel_call(
        second_send_body,
        (shape((share, extended), BF16), shape((share, extended), F32)),
        [vmem_spec()] * 2,
        [pltpu.VMEM((rows, extended), F32)],
    )(keep, arrived)
    arrived = swapped(send, "dp", 2)
    (block_3,) = fetched(send, (3, 0, 8))
    group = heads_here // key_heads
    positions = n_tensor * span + 16
    owners = lax.axis_size("dp")
    heads, block_2 = kernel_call(
        functools.partial(attend_body, rows_dev),
        (shape((share, query_columns), BF16), weight_block(6)),
        [vmem_spec()] * 13 + [any_spec(), hbm_spec()],
        [
            pltpu.VMEM((owners, share, query_columns // owners), F32),
            pltpu.VMEM((2, owners, share, 2 * key_columns // owners), F32),
            pltpu.VMEM((key_heads, group * share, head_dim), F32),
            pltpu.VMEM((key_heads, group * share, head_dim), F32),
            pltpu.VMEM((rows_dev * key_heads, positions, head_dim), BF16),
            pltpu.VMEM((rows_dev * key_heads, positions, head_dim), BF16),
            fetch_sems,
        ],
        moved=10e6,
    )(length, trig, kept, arrived, *all_factors, near, *far, far_late, block_3, w_out)

    heads_x = swapped(heads, "dp", 2)
    heads_core = swapped(heads, "dp", 1)
    last_2, block_1 = fetched(heads, (2, 6, 2), (1, 0, 4))
    heads_x, _ = lax.optimization_barrier((heads_x, block_1))
    heads_both = swapped(heads_x, "dp", 1)
    message = shape((both, part + rank), BF16)
    summed = shape((both, part + rank), F32)
    send_3, low, all_rows, last_1 = kernel_call(
        functools.partial(far_output_body, 1, 4 * eighth),
        (
            message,
            shape((both, rank), F32),
            shape((both, w_out.shape[0]), BF16),
            weight_block(4),
        ),
        [vmem_spec()] * 9 + [any_spec(), hbm_spec()],
        [pltpu.VMEM((both, w_out.shape[0]), F32), fetch_sems],
        mib=8,
        moved=10e6,
    )(heads, heads_core, heads_x, heads_both, *all_factors, block_3, block_1, w_out)
    far_3 = swapped(send_3, "tensor", 3)

    def next_output(*weights):
        return kernel_call(
            next_output_body,
            (message,),
            [vmem_spec()] * (2 + len(weights)),
            mib=8,
            moved=40e6,
        )(all_rows, low, *weights)[0]

    def added(total, far_part, moved):
        return kernel_call(add_far_body, (summed,), [vmem_spec()] * 2, mib=8, moved=moved)(
            total, far_part
        )[0]

    far_2 = swapped(next_output(block_2, last_2), "tensor", 2)
    far_1 = swapped(next_output(block_1, last_1), "tensor", 1)
    (total,) = kernel_call(
        own_output_body,
        (summed,),
        [vmem_spec(), vmem_spec(), hbm_spec()],
        [weight_block(8), pltpu.SemaphoreType.DMA((8,))],
        mib=12,
        moved=40e6,
    )(all_rows, low, w_out)
    total = added(added(total, far_3, 40e6), far_2, 40e6)
    (done,) = kernel_call(
        functools.partial(finish_body, rows_dev),
        (shape((both, part), BF16),),
        [vmem_spec()] * 3,
        mib=8,
    )(total, far_1, b_out)
    parts = [done] + [swapped(done, "tensor", mask) for mask in (1, 2, 3)]
    return kernel_call(
        place_body,
        (shape((rows, out_columns), BF16), shape((rows, out_columns), BF16)),
        [vmem_spec()] * 4,
        [pltpu.SemaphoreType.DMA((4, 2))],
        out_specs=(hbm_spec(), hbm_spec()),
    )(*parts)


def takes_joined(mesh):
    return mesh.shape["dp"] == 4 and mesh.shape["tensor"] == 4


def solution(mesh):
    in_specs = (
        P("groups", "dp"),
        P("groups", "dp"),
        P("dp"),
        P("dp", "tensor"),
        P("dp", "tensor"),
        P("dp", "tensor"),
        P("tensor", "dp"),
        P(("dp", "tensor"), None),
        P(None, ("tensor", "dp")),
        P(("dp", "tensor"), None),
        P(None, ("tensor", "dp")),
        P(("dp", "tensor"), None),
        P(None, ("tensor", "dp")),
        P(("tensor", "dp"), None),
        P(None, ("dp", "tensor")),
        P(("groups", "dp"), None, "tensor", None),
        P(("groups", "dp"), None, "tensor", None),
        P(("groups", "dp")),
    )
    out_specs = (P("groups", "dp"), P("groups", "dp"))
    return jax.shard_map(
        on_device_joined if takes_joined(mesh) else on_device,
        mesh=mesh,
        in_specs=in_specs,
        out_specs=out_specs,
        check_vma=False,
    )
```

```python
import functools
import math

import jax
import jax.numpy as jnp
import numpy as np
from jax import lax
from jax.experimental import pallas as pl
from jax.experimental.pallas import tpu as pltpu
from jax.sharding import PartitionSpec as P

D = 16384


ADAPTER_SCALE = 2.0
ROPE_BASE = 500000.0
EPS = 1e-05
MASKED_FILLER = -1e30
BF16 = jnp.bfloat16
F32 = jnp.float32


def joined_2(part, axis, combine):
    gathered = jax.tree.map(lambda a: lax.all_gather(a, axis), part)

    def take(source):
        return jax.tree.map(lambda a: lax.dynamic_index_in_dim(a, source, 0, False), gathered)

    return lax.fori_loop(
        1, lax.axis_size(axis), lambda source, state: combine(state, take(source)), take(0)
    )


def merge_weight(frozen_weight, factor_in, factor_out):
    adapter_update = jnp.dot(factor_in, factor_out, preferred_element_type=jnp.float32)
    return (frozen_weight.astype(jnp.float32) + ADAPTER_SCALE * adapter_update).astype(jnp.bfloat16)


def rotary(vectors, positions_now):
    half_dim = vectors.shape[-1] // 2
    frequency = ROPE_BASE ** (-jnp.arange(half_dim, dtype=jnp.float32) / half_dim)
    angles = positions_now.astype(jnp.float32)[:, None] * frequency[None, :]
    cosine = jnp.cos(angles)[:, None, :]
    sine_part = jnp.sin(angles)[:, None, :]
    lower = vectors[..., :half_dim]
    upper = vectors[..., half_dim:]
    return jnp.concatenate(
        [lower * cosine - upper * sine_part, upper * cosine + lower * sine_part], axis=-1
    )


def combine_partial(earlier, later):
    highest = jnp.maximum(earlier[0], later[0])
    weight_a = jnp.exp(earlier[0] - highest)
    weight_b = jnp.exp(later[0] - highest)
    return (
        highest,
        earlier[1] * weight_a + later[1] * weight_b,
        earlier[2] * weight_a[..., None] + later[2] * weight_b[..., None],
    )


def on_device(
    hidden_first,
    hidden_second,
    norm_gain,
    query_weight,
    w_key,
    w_value,
    w_out,
    a_query,
    b_query,
    a_key,
    b_key,
    a_value,
    b_value,
    a_out,
    b_out,
    cache_keys,
    cache_values,
    lengths,
):
    tensor_parts = (
        lax.all_gather(a_query, "tensor", axis=0, tiled=True),
        lax.all_gather(a_key, "tensor", axis=0, tiled=True),
        lax.all_gather(a_value, "tensor", axis=0, tiled=True),
        lax.all_gather(b_out, "tensor", axis=1, tiled=True),
    )
    data_parts = (
        lax.all_gather(b_query, "dp", axis=1, tiled=True),
        lax.all_gather(b_key, "dp", axis=1, tiled=True),
        lax.all_gather(b_value, "dp", axis=1, tiled=True),
        lax.all_gather(a_out, "dp", axis=0, tiled=True),
    )
    merged_qkv = jnp.concatenate(
        [
            merge_weight(query_weight, tensor_parts[0], data_parts[0]),
            merge_weight(w_key, tensor_parts[1], data_parts[1]),
            merge_weight(w_value, tensor_parts[2], data_parts[2]),
        ],
        axis=1,
    )
    merged_output = merge_weight(w_out, data_parts[3], tensor_parts[3])
    n_tensor = lax.axis_size("tensor")
    tensor_index = lax.axis_index("tensor")
    rows_dev, key_value_heads, cache_span, head_dim = cache_keys.shape
    query_cols = query_weight.shape[1]
    key_cols = w_key.shape[1]
    joint_cols = query_cols + 2 * key_cols
    heads_here = query_cols // head_dim
    all_heads = heads_here * n_tensor
    group_size = all_heads // key_value_heads
    score_scale = 1.0 / math.sqrt(head_dim)
    cache_positions = tensor_index * cache_span + jnp.arange(cache_span, dtype=jnp.int32)
    cache_valid = cache_positions[None, :] < lengths[:, None]
    first_owner = tensor_index == 0
    fresh_keys = []
    fresh_values = []
    results = []
    for step_index, hidden in enumerate((hidden_first, hidden_second)):
        values_f = hidden.astype(jnp.float32)
        squares = lax.psum(jnp.sum(values_f * values_f, axis=1), "dp")
        normed = (
            values_f * lax.rsqrt(squares / D + EPS)[:, None] * norm_gain.astype(jnp.float32)
        ).astype(jnp.bfloat16)
        projected = lax.psum_scatter(
            jnp.dot(normed, merged_qkv, preferred_element_type=jnp.float32),
            "dp",
            scatter_dimension=0,
            tiled=True,
        ).astype(jnp.bfloat16)
        joined = lax.all_gather(projected, "tensor", axis=1, tiled=True).reshape(
            rows_dev, n_tensor, joint_cols
        )
        queries = joined[:, :, :query_cols].reshape(rows_dev, all_heads, head_dim)
        key_now = joined[:, :, query_cols : query_cols + key_cols].reshape(
            rows_dev, key_value_heads, head_dim
        )
        value_now = joined[:, :, query_cols + key_cols :].reshape(
            rows_dev, key_value_heads, head_dim
        )
        positions_now = lengths + step_index
        queries = rotary(queries.astype(jnp.float32), positions_now).astype(jnp.bfloat16)
        queries = queries.reshape(rows_dev, key_value_heads, group_size, head_dim)
        fresh_keys.append(rotary(key_now.astype(jnp.float32), positions_now).astype(jnp.bfloat16))
        fresh_values.append(value_now)
        cache_scores = (
            jnp.einsum("rkgd,rksd->rkgs", queries, cache_keys, preferred_element_type=jnp.float32)
            * score_scale
        )
        cache_scores = jnp.where(cache_valid[:, None, None, :], cache_scores, MASKED_FILLER)
        new_scores = (
            jnp.einsum(
                "rkgd,rknd->rkgn",
                queries,
                jnp.stack(fresh_keys, axis=2),
                preferred_element_type=jnp.float32,
            )
            * score_scale
        )
        new_scores = jnp.where(first_owner, new_scores, MASKED_FILLER)
        highest = jnp.maximum(jnp.max(cache_scores, axis=-1), jnp.max(new_scores, axis=-1))
        cache_weights = jnp.where(
            cache_valid[:, None, None, :], jnp.exp(cache_scores - highest[..., None]), 0.0
        )
        new_weights = jnp.where(first_owner, jnp.exp(new_scores - highest[..., None]), 0.0)
        totals = jnp.sum(cache_weights, axis=-1) + jnp.sum(new_weights, axis=-1)
        weighted = jnp.einsum(
            "rkgs,rksd->rkgd", cache_weights, cache_values, preferred_element_type=jnp.float32
        )
        weighted = weighted + jnp.einsum(
            "rkgn,rknd->rkgd",
            new_weights,
            jnp.stack(fresh_values, axis=2),
            preferred_element_type=jnp.float32,
        )
        highest = highest.reshape(rows_dev, all_heads)
        totals = totals.reshape(rows_dev, all_heads)
        weighted = weighted.reshape(rows_dev, all_heads, head_dim)
        high_all, total_all, weighted_all = joined_2(
            (highest, totals, weighted), "tensor", combine_partial
        )
        normalized = weighted_all / total_all[..., None]
        own_heads = lax.dynamic_slice_in_dim(normalized, tensor_index * heads_here, heads_here, 1)
        heads = own_heads.reshape(rows_dev, query_cols).astype(jnp.bfloat16)
        out_terms = jnp.dot(
            lax.all_gather(heads, "dp", axis=0, tiled=True),
            merged_output,
            preferred_element_type=jnp.float32,
        )
        attn_out = lax.psum(out_terms, "tensor").astype(jnp.bfloat16)
        results.append(attn_out)
    return (results[0], results[1])

def swapped(array, axis, mask):
    size = lax.axis_size(axis)
    return lax.ppermute(array, axis, [(k, k ^ mask) for k in range(size)])


def vmem_spec():
    return pl.BlockSpec(memory_space=pltpu.VMEM)


def any_spec():
    return pl.BlockSpec(memory_space=pl.ANY)


def hbm_spec():
    return pl.BlockSpec(memory_space=pltpu.HBM)


def in_hbm(*arrays):
    return [pltpu.with_memory_space_constraint(array, pltpu.HBM) for array in arrays]


def cost(moved):
    return pl.CostEstimate(flops=0, bytes_accessed=int(moved), transcendentals=0)


def kernel_call(body, outs, in_specs, scratch=(), mib=12, out_specs=None, moved=0):
    return pl.pallas_call(
        body,
        out_shape=outs,
        in_specs=in_specs,
        out_specs=out_specs or tuple(vmem_spec() for _ in outs),
        scratch_shapes=list(scratch),
        cost_estimate=cost(moved),
        compiler_params=pltpu.CompilerParams(vmem_limit_bytes=mib << 20),
    )


def aligned(start, size, unit):
    return pl.ds(pl.multiple_of(start, unit), size)


def split_sum(total, width):
    high = total.astype(BF16).astype(F32)
    rest = total - high
    middle = rest.astype(BF16).astype(F32)
    low = rest - middle
    lane = lax.broadcasted_iota(jnp.int32, (total.shape[0], width), 1)
    return jnp.where(
        lane == 0, high, jnp.where(lane == 1, middle, jnp.where(lane == 2, low, 0.0))
    )


def low_places(shape, rows, place):
    blocks, span, _ = shape
    first = blocks - -(-3 * rows // span)
    for part in range(0, rows, 16):
        flat = place * rows + part
        yield first + flat // span, flat % span, part


def prepare_body(
    rows_dev,
    first_ref,
    second_ref,
    gain_ref,
    a_query_ref,
    a_key_ref,
    a_value_ref,
    keys_ref,
    values_ref,
    b_query_ref,
    b_key_ref,
    b_value_ref,
    a_out_ref,
    _,
    scaled_ref,
    squares_ref,
    low_ref,
    near,
    far_1,
    far_2,
    far_3,
    far_late,
    factors_ref,
    hidden,
    gain_held,
    a_held,
    sems,
):
    tensor_index = lax.axis_index("tensor")
    heads_here = keys_ref.shape[1] // lax.axis_size("tensor")
    rank = a_query_ref.shape[1]
    wide = b_query_ref.shape[1]
    narrow = b_key_ref.shape[0]

    def begun(group, pairs):
        copies = [pltpu.make_async_copy(*pair, sems.at[group]) for pair in pairs]
        for copy in copies:
            copy.start()
        return copies

    inputs = begun(
        0, [(first_ref, hidden.at[0]), (second_ref, hidden.at[1]), (gain_ref, gain_held)]
    )
    inputs += begun(
        1,
        [(ref, a_held.at[place]) for place, ref in enumerate((a_query_ref, a_key_ref, a_value_ref))],
    )
    moves = []
    for mask, far in enumerate((near, far_1, far_2, far_3)):
        head = jnp.bitwise_xor(tensor_index, mask) * heads_here
        for kind, cache in enumerate((keys_ref, values_ref)):
            for row in range(rows_dev):
                late = mask == 3 and (kind == 1 or row == rows_dev - 1)
                if late:
                    start = (row if kind == 1 else rows_dev) * heads_here
                else:
                    start = (kind * rows_dev + row) * heads_here
                target = far_late if late else far
                moves.append(
                    (cache.at[row, pl.ds(head, heads_here)], target.at[pl.ds(start, heads_here)])
                )
    moves.append((b_query_ref, factors_ref.at[:, pl.ds(0, wide)]))
    for place, ref in enumerate((b_key_ref, b_value_ref)):
        moves.append((ref, factors_ref.at[pl.ds(place * narrow, narrow), pl.ds(wide, rank)]))
    for piece in range(a_out_ref.shape[0] // rank):
        moves.append(
            (
                a_out_ref.at[pl.ds(piece * rank, rank)],
                factors_ref.at[:, pl.ds(wide + (piece + 1) * rank, rank)],
            )
        )
    moves = begun(2, moves)
    @pl.when(tensor_index >= 0)
    def scaled():
        for copy in inputs[:3]:
            copy.wait()
        rows, width = first_ref.shape
        pieces = []
        sums = [jnp.zeros((rows, 128), F32), jnp.zeros((rows, 128), F32)]

        def by_owner(pair):
            ordered = []
            for owner in range(rows // rows_dev):
                for part in pair:
                    ordered.append(part[owner * rows_dev : (owner + 1) * rows_dev])
            return jnp.concatenate(ordered, axis=0)

        for piece in range(width // 128):
            columns = slice(piece * 128, (piece + 1) * 128)
            steps = [hidden[step, :, columns].astype(F32) for step in range(2)]
            sums = [total + step * step for total, step in zip(sums, steps)]
            gain = gain_held[piece : piece + 1, :].astype(F32)
            scaled_ref[:, columns] = by_owner([step * gain for step in steps]).astype(BF16)
        squares_ref[...] = by_owner(sums)
        for copy in inputs[3:]:
            copy.wait()
        depth = a_query_ref.shape[0]
        own = scaled_ref[:, aligned(tensor_index * depth, depth, 128)]
        low_rows = scaled_ref.shape[0]
        for place in range(3):
            low = jnp.dot(own, a_held[place], preferred_element_type=F32)
            low_ref[:, place * rank : (place + 1) * rank] = low
            for far in (far_1, far_2, far_3):
                for at, row, part in low_places(far.shape, low_rows, place):
                    far[at, row : row + 16, :] = low[part : part + 16].astype(BF16)

    for copy in moves:
        copy.wait()


def project_body(
    rows_dev,
    lengths_ref,
    scaled_ref,
    query_ref,
    key_ref,
    value_ref,
    sums_ref,
    trig_ref,
    length_ref,
    ring,
    lengths_held,
    ring_sem,
    held_sem,
):
    slots, depth, columns = ring.shape
    chunks = query_ref.shape[0] // depth

    def fetch(chunk):
        slot = chunk % slots
        return pltpu.make_async_copy(
            query_ref.at[pl.ds(chunk * depth, depth)], ring.at[slot], ring_sem.at[slot]
        )

    for chunk in range(min(slots, chunks)):
        fetch(chunk).start()
    lengths_copy = pltpu.make_async_copy(lengths_ref, lengths_held, held_sem.at[0])
    lengths_copy.start()
    lengths_copy.wait()
    shape = length_ref.shape
    half = shape[1] // 2
    row = lax.broadcasted_iota(jnp.int32, shape, 0)
    lane = lax.broadcasted_iota(jnp.int32, shape, 1)
    length = jnp.zeros(shape, jnp.int32)
    for place in range(rows_dev):
        length = length + jnp.where(row % rows_dev == place, lengths_held[place], 0)
    length_ref[...] = length
    exponent = (lane % half).astype(F32) / half
    frequency = jnp.exp(exponent * (-math.log(ROPE_BASE)))
    angles = (length + row // rows_dev).astype(F32) * frequency
    sine = jnp.sin(angles)
    trig_ref[: shape[0], :] = jnp.cos(angles)
    trig_ref[shape[0] :, :] = jnp.where(lane < half, -sine, sine)
    place = columns
    for held in (key_ref, value_ref):
        sums_ref[:, place : place + held.shape[1]] = jnp.dot(
            scaled_ref[...], held[...], preferred_element_type=F32
        )
        place += held.shape[1]
    for chunk in range(chunks):
        fetch(chunk).wait()
        term = jnp.dot(
            scaled_ref[:, chunk * depth : (chunk + 1) * depth],
            ring[chunk % slots],
            preferred_element_type=F32,
        )
        if chunk == 0:
            sums_ref[:, :columns] = term
        else:
            sums_ref[:, :columns] += term
        if chunk + slots < chunks:
            fetch(chunk + slots).start()


def first_send_body(sums_ref, low_ref, squares_ref, far_1, far_2, far_3, send_ref, keep_ref, full):
    core = lax.rem(lax.axis_index("dp"), 2)
    columns = sums_ref.shape[1]
    rows, low_columns = low_ref.shape
    rank = low_columns // 3
    full[:, :columns] = sums_ref[...]
    for place in range(3):
        low = low_ref[:, place * rank : (place + 1) * rank]
        for far in (far_1, far_2, far_3):
            low = low + jnp.concatenate(
                [
                    far[at, row : row + 16, :].astype(F32)
                    for at, row, _ in low_places(far.shape, rows, place)
                ],
                axis=0,
            )
        full[:, columns + place * rank : columns + (place + 1) * rank] = low
    full[:, columns + low_columns :] = split_sum(
        jnp.sum(squares_ref[...], axis=1, keepdims=True), 128
    )
    share = rows // 4
    other = 1 - core
    send_ref[...] = jnp.concatenate(
        [
            full[aligned(other * share, share, 8), :],
            full[aligned((other + 2) * share, share, 8), :],
        ],
        axis=0,
    ).astype(BF16)
    keep_ref[:share, :] = full[aligned(core * share, share, 8), :]
    keep_ref[share:, :] = full[aligned((core + 2) * share, share, 8), :]


def second_send_body(keep_ref, arrived_ref, send_ref, kept_ref, full):
    chip = lax.axis_index("dp") // 2
    full[...] = keep_ref[...] + arrived_ref[...].astype(F32)
    full[:, -128:] = split_sum(jnp.sum(full[:, -128:], axis=1, keepdims=True), 128)
    share = full.shape[0] // 2
    send_ref[...] = full[aligned((1 - chip) * share, share, 8), :].astype(BF16)
    kept_ref[...] = full[aligned(chip * share, share, 8), :]


def attend_body(
    rows_dev,
    length_ref,
    trig_ref,
    kept_ref,
    arrived_ref,
    factors_0,
    factors_1,
    factors_2,
    factors_3,
    near,
    far_1,
    far_2,
    far_3,
    far_late,
    _,
    weight_ref,
    heads_ref,
    block_ref,
    low_query,
    low_narrow,
    turned,
    mixed,
    keys_all,
    values_all,
    sems,
):
    dp_index = lax.axis_index("dp")
    tensor_index = lax.axis_index("tensor")
    copies = fetch_copies(weight_ref, jnp.bitwise_xor(tensor_index, 2), 0, block_ref, sems)
    for copy in copies:
        copy.start()
    @pl.when(dp_index >= 0)
    def attended():
        rows = 2 * rows_dev
        span, head_dim = near.shape[1:]
        key_heads = keys_all.shape[0] // rows_dev
        query_columns = heads_ref.shape[1]
        heads = query_columns // head_dim
        group = heads // key_heads
        sources = lax.axis_size("tensor")
        rank = factors_0.shape[0]
        owners = lax.axis_size("dp")
        wide = query_columns // owners
        narrow = key_heads * head_dim // owners

        for place in range(rows_dev * key_heads):
            last = place - (rows_dev - 1) * key_heads
            for mask, block in enumerate((near, far_1, far_2, far_3)):
                rows_here = slice(mask * span, (mask + 1) * span)
                key_block, value_block = block, block
                key_place, value_place = place, rows_dev * key_heads + place
                if mask == 3:
                    value_block, value_place = far_late, place
                    if last >= 0:
                        key_block, key_place = far_late, rows_dev * key_heads + last
                keys_all[place, rows_here, :] = key_block[key_place]
                values_all[place, rows_here, :] = value_block[value_place]

        total = kept_ref[...] + arrived_ref[...].astype(F32)
        joint = query_columns + 2 * key_heads * head_dim
        squares = jnp.sum(total[:, -128:], axis=1, keepdims=True)
        scale = lax.rsqrt(squares / D + EPS)
        lows = [
            total[:, joint + place * rank : joint + (place + 1) * rank].astype(BF16)
            for place in range(3)
        ]
        for mask, factors in enumerate((factors_0, factors_1, factors_2, factors_3)):
            owner = jnp.bitwise_xor(dp_index, mask)
            low_query[owner] = jnp.dot(lows[0], factors[:, :wide], preferred_element_type=F32)
            pair = factors[:, wide : wide + 2 * narrow]
            for place in range(2):
                low_narrow[place, owner] = lax.dot_general(
                    lows[place + 1], pair, (((1,), (1,)), ((), ())), preferred_element_type=F32
                )
        cosine = trig_ref[:rows, :]
        sine = trig_ref[rows:, :]

        def turn(vector):
            return vector * cosine + pltpu.roll(vector, head_dim // 2, 1) * sine

        def rounded(vector):
            return vector.astype(BF16).astype(F32)

        for head in range(heads):
            column = head * head_dim
            owner, inner = column // wide, column % wide
            vector = (
                total[:, column : column + head_dim]
                + ADAPTER_SCALE * low_query[owner, :, inner : inner + head_dim]
            )
            start = (head % group) * rows
            turned[head // group, start : start + rows, :] = turn(rounded(vector * scale))

        lane = lax.broadcasted_iota(jnp.int32, (rows, head_dim), 1)
        per_head = head_dim // narrow
        fresh = [[], []]
        for place in range(2):
            for head in range(key_heads):
                low = jnp.zeros((rows, head_dim), F32)
                for part in range(per_head):
                    piece = low_narrow[place, head * per_head + part]
                    shift = (part * narrow - place * narrow) % (2 * narrow)
                    if shift:
                        piece = pltpu.roll(piece, shift, 1)
                    low = jnp.where(lane // narrow == part, piece, low)
                column = query_columns + place * key_heads * head_dim + head * head_dim
                vector = rounded(
                    (total[:, column : column + head_dim] + ADAPTER_SCALE * low) * scale
                )
                fresh[place].append(turn(vector) if place == 0 else vector)

        cached = sources * span
        width = keys_all.shape[1]
        column = lax.broadcasted_iota(jnp.int32, (1, width), 1)
        position = jnp.where(column == cached, -1, 1 << 30)
        for mask in range(sources):
            base = jnp.bitwise_xor(tensor_index, mask) * span
            inside = (column >= mask * span) & (column < (mask + 1) * span)
            position = jnp.where(inside, column - mask * span + base, position)
        step = lax.broadcasted_iota(jnp.int32, (2 * group, width), 0) % 2
        second = (step == 1) & (
            lax.broadcasted_iota(jnp.int32, (2 * group, width), 1) == cached + 1
        )
        score_scale = 1.0 / math.sqrt(head_dim)
        for row in range(rows_dev):
            valid = (position < length_ref[row : row + 1, :1]) | second
            for head in range(key_heads):
                place = row * key_heads + head
                for joined, parts in ((keys_all, fresh[0]), (values_all, fresh[1])):
                    joined[place, cached:, :] = jnp.concatenate(
                        [
                            parts[head][row : row + 1],
                            parts[head][rows_dev + row : rows_dev + row + 1],
                            jnp.zeros((width - cached - 2, head_dim), F32),
                        ],
                        axis=0,
                    ).astype(BF16)
                query = turned[head, pl.ds(row, 2 * group, stride=rows_dev), :].astype(BF16)
                scores = (
                    lax.dot_general(
                        query,
                        keys_all[place],
                        (((1,), (1,)), ((), ())),
                        preferred_element_type=F32,
                    )
                    * score_scale
                )
                scores = jnp.where(valid, scores, MASKED_FILLER)
                highest = jnp.max(scores, axis=1, keepdims=True)
                weights = jnp.where(valid, jnp.exp(scores - highest), 0.0)
                totals = jnp.sum(weights, axis=1, keepdims=True)
                weighted = jnp.dot(
                    weights.astype(BF16), values_all[place], preferred_element_type=F32
                )
                mixed[head, pl.ds(row, 2 * group, stride=rows_dev), :] = weighted / totals
        for head in range(heads):
            start = (head % group) * rows
            heads_ref[:, head * head_dim : (head + 1) * head_dim] = mixed[
                head // group, start : start + rows, :
            ].astype(BF16)

    for copy in copies:
        copy.wait()


def fetch_copies(weight_ref, target, first, block_ref, sems):
    depth, part = block_ref.shape
    pieces = sems.shape[0]
    rows = depth // pieces
    return [
        pltpu.make_async_copy(
            weight_ref.at[
                pl.ds(first + piece * rows, rows), aligned(target * part, part, 128)
            ],
            block_ref.at[pl.ds(piece * rows, rows)],
            sems.at[piece],
        )
        for piece in range(pieces)
    ]


def fetch_body(pieces, weight_ref, _, *blocks_and_sems):
    *blocks, sems = blocks_and_sems
    copies = []
    for place, ((mask, first), block_ref) in enumerate(zip(pieces, blocks)):
        target = jnp.bitwise_xor(lax.axis_index("tensor"), mask)
        copies += fetch_copies(weight_ref, target, first, block_ref, sems.at[place])
    for copy in copies:
        copy.start()
    for copy in copies:
        copy.wait()


def product(rows_ref, *blocks):
    width = math.gcd(blocks[0].shape[1], 512)
    results = []
    for start in range(0, blocks[0].shape[1], width):
        first, result = 0, None
        for block in blocks:
            depth = block.shape[0]
            term = jnp.dot(
                rows_ref[:, first : first + depth],
                block[:, start : start + width],
                preferred_element_type=F32,
            )
            result = term if result is None else result + term
            first += depth
        results.append(result)
    return jnp.concatenate(results, axis=1)


def far_output_body(
    mask,
    first,
    heads_0,
    heads_1,
    heads_2,
    heads_3,
    factors_0,
    factors_1,
    factors_2,
    factors_3,
    block_ref,
    _,
    weight_ref,
    send_ref,
    low_ref,
    all_rows,
    fetched_ref,
    wide_rows,
    sems,
):
    dp_index = lax.axis_index("dp")
    target = jnp.bitwise_xor(lax.axis_index("tensor"), mask)
    copies = fetch_copies(weight_ref, target, first, fetched_ref, sems)
    for copy in copies:
        copy.start()
    @pl.when(dp_index >= 0)
    def multiplied():
        share = heads_0.shape[0]
        for distance, part in enumerate((heads_0, heads_1, heads_2, heads_3)):
            owner = jnp.bitwise_xor(dp_index, distance)
            wide_rows[aligned(owner * share, share, 8), :] = part[...].astype(F32)
        all_rows[...] = wide_rows[...].astype(BF16)
        rank = factors_0.shape[0]
        block = all_rows.shape[1] // lax.axis_size("dp")
        pieces = block // rank
        base = factors_0.shape[1] - pieces * rank
        low = jnp.zeros((all_rows.shape[0], rank), F32)
        for distance, factors in enumerate((factors_0, factors_1, factors_2, factors_3)):
            owner = jnp.bitwise_xor(dp_index, distance)
            for piece in range(pieces):
                low = low + jnp.dot(
                    all_rows[:, aligned(owner * block + piece * rank, rank, 128)],
                    factors[:, base + piece * rank : base + (piece + 1) * rank],
                    preferred_element_type=F32,
                )
        low_ref[...] = low
        part = block_ref.shape[1]
        send_ref[:, :part] = product(all_rows, block_ref).astype(BF16)
        send_ref[:, part:] = low.astype(BF16)

    for copy in copies:
        copy.wait()


def next_output_body(all_rows, low_ref, *blocks_and_result):
    *blocks, result_ref = blocks_and_result
    part = blocks[0].shape[1]
    result_ref[:, :part] = product(all_rows, *blocks).astype(result_ref.dtype)
    result_ref[:, part:] = low_ref[...].astype(result_ref.dtype)


def own_output_body(all_rows, low_ref, first_ref, weight_ref, result_ref, held, sems):
    tensor_index = lax.axis_index("tensor")
    done = first_ref.shape[0]
    copies = fetch_copies(weight_ref, tensor_index, done, held, sems)
    for copy in copies:
        copy.start()
    part = held.shape[1]
    rows = held.shape[0] // len(copies)

    @pl.when(tensor_index >= 0)
    def multiplied():
        result_ref[:, part:] = low_ref[...]
        result_ref[:, :part] = product(all_rows, first_ref)

    for piece, copy in enumerate(copies):
        copy.wait()
        here = slice(piece * rows, (piece + 1) * rows)
        result_ref[:, :part] += jnp.dot(
            all_rows[:, done + piece * rows : done + (piece + 1) * rows],
            held[here, :],
            preferred_element_type=F32,
        )


def add_far_body(keep_ref, far, sum_ref):
    sum_ref[...] = keep_ref[...] + far[...].astype(F32)


def finish_body(rows_dev, sum_ref, far_1, b_out_ref, part_ref):
    total = sum_ref[...] + far_1[...].astype(F32)
    part = b_out_ref.shape[1]
    low = total[:, part:].astype(BF16)
    result = total[:, :part] + ADAPTER_SCALE * jnp.dot(
        low, b_out_ref[...], preferred_element_type=F32
    )
    pieces = []
    for step in range(2):
        for owner in range(result.shape[0] // (2 * rows_dev)):
            start = (2 * owner + step) * rows_dev
            pieces.append(result[start : start + rows_dev])
    part_ref[...] = jnp.concatenate(pieces, axis=0).astype(BF16)


def place_body(part_0, part_1, part_2, part_3, first_ref, second_ref, sems):
    tensor_index = lax.axis_index("tensor")
    rows = first_ref.shape[0]
    copies = []
    for mask, part in enumerate((part_0, part_1, part_2, part_3)):
        width = part.shape[1]
        columns = aligned(jnp.bitwise_xor(tensor_index, mask) * width, width, 128)
        for step, target in enumerate((first_ref, second_ref)):
            copies.append(
                pltpu.make_async_copy(
                    part.at[pl.ds(step * rows, rows)],
                    target.at[:, columns],
                    sems.at[mask, step],
                )
            )
    for copy in copies:
        copy.start()
    for copy in copies:
        copy.wait()


def on_device_joined(
    hidden_first,
    hidden_second,
    norm_gain,
    query_weight,
    w_key,
    w_value,
    w_out,
    a_query,
    b_query,
    a_key,
    b_key,
    a_value,
    b_value,
    a_out,
    b_out,
    cache_keys,
    cache_values,
    lengths,
):
    shape = jax.ShapeDtypeStruct
    rows, width = hidden_first.shape
    rows_dev, all_key_heads, span, head_dim = cache_keys.shape
    n_tensor = lax.axis_size("tensor")
    key_heads = all_key_heads // n_tensor
    rank = a_query.shape[1]
    query_columns = query_weight.shape[1]
    key_columns = w_key.shape[1]
    joint = query_columns + 2 * key_columns
    both = 2 * rows
    share = 2 * rows_dev
    low_columns = 3 * rank
    blocks = 2 * rows_dev * key_heads
    low_blocks = -(-3 * both // span)
    pack_columns = b_query.shape[1] + rank + a_out.shape[0]

    scaled, squares, low, near, far_1, far_2, far_3, far_late, factors = kernel_call(
        functools.partial(prepare_body, rows_dev),
        (
            shape((both, width), BF16),
            shape((both, 128), F32),
            shape((both, low_columns), F32),
            shape((blocks, span, head_dim), BF16),
            shape((blocks + low_blocks, span, head_dim), BF16),
            shape((blocks + low_blocks, span, head_dim), BF16),
            shape((blocks // 2 - key_heads + low_blocks, span, head_dim), BF16),
            shape((blocks // 2 + key_heads, span, head_dim), BF16),
            shape((rank, pack_columns), BF16),
        ),
        [hbm_spec()] * 13,
        [
            pltpu.VMEM((2, rows, width), BF16),
            pltpu.VMEM((width // 128, 128), BF16),
            pltpu.VMEM((3,) + a_query.shape, BF16),
            pltpu.SemaphoreType.DMA((3,)),
        ],
        moved=60e6,
    )(
        *in_hbm(
            hidden_first,
            hidden_second,
            norm_gain.reshape(width // 128, 128),
            a_query,
            a_key,
            a_value,
            cache_keys,
            cache_values,
            b_query,
            b_key.T,
            b_value.T,
            a_out,
            w_out,
        )
    )
    far = [swapped(part, "tensor", mask) for mask, part in ((1, far_1), (2, far_2), (3, far_3))]
    factors_x = swapped(factors, "dp", 2)
    factors_core = swapped(factors, "dp", 1)

    depth = math.gcd(width, 256)
    sums, trig, length = kernel_call(
        functools.partial(project_body, rows_dev),
        (
            shape((both, joint), F32),
            shape((2 * share, head_dim), F32),
            shape((share, head_dim), jnp.int32),
        ),
        [hbm_spec(), vmem_spec(), hbm_spec(), vmem_spec(), vmem_spec()],
        [
            pltpu.VMEM((4, depth, query_columns), BF16),
            pltpu.SMEM((rows_dev,), jnp.int32),
            pltpu.SemaphoreType.DMA((4,)),
            pltpu.SemaphoreType.DMA((1,)),
        ],
        moved=2 * width * joint,
        mib=16,
    )(*in_hbm(lengths), scaled, *in_hbm(query_weight), w_key, w_value)
    heads_here = query_columns // head_dim
    out_columns = w_out.shape[1]
    part = out_columns // n_tensor
    eighth = w_out.shape[0] // 8

    def weight_block(eighths):
        return pltpu.VMEM((eighths * eighth, part), BF16)

    (w_out,) = in_hbm(w_out)
    fetch_sems = pltpu.SemaphoreType.DMA((4,))

    def fetched(after, *pieces):
        return kernel_call(
            functools.partial(
                fetch_body, [(mask, first * eighth) for mask, first, _ in pieces]
            ),
            tuple(weight_block(eighths) for _, _, eighths in pieces),
            [hbm_spec(), any_spec()],
            [pltpu.SemaphoreType.DMA((len(pieces), 4))],
            mib=4,
            moved=2 * sum(eighths for _, _, eighths in pieces) * eighth * part,
        )(w_out, after)

    extended = joint + low_columns + 128
    send, keep = kernel_call(
        first_send_body,
        (shape((rows, extended), BF16), shape((rows, extended), F32)),
        [vmem_spec()] * 6,
        [pltpu.VMEM((both, extended), F32)],
    )(sums, low, squares, *far)
    factors_x, far_late, send = lax.optimization_barrier((factors_x, far_late, send))
    far_late = swapped(far_late, "tensor", 3)
    factors_both = swapped(factors_x, "dp", 1)
    all_factors = (factors, factors_core, factors_x, factors_both)
    arrived = swapped(send, "dp", 1)
    send, kept = kernel_call(
        second_send_body,
        (shape((share, extended), BF16), shape((share, extended), F32)),
        [vmem_spec()] * 2,
        [pltpu.VMEM((rows, extended), F32)],
    )(keep, arrived)
    arrived = swapped(send, "dp", 2)
    block_3, own_first = fetched(send, (3, 0, 8), (0, 0, 2))
    group = heads_here // key_heads
    positions = n_tensor * span + 16
    owners = lax.axis_size("dp")
    heads, block_2 = kernel_call(
        functools.partial(attend_body, rows_dev),
        (shape((share, query_columns), BF16), weight_block(6)),
        [vmem_spec()] * 13 + [any_spec(), hbm_spec()],
        [
            pltpu.VMEM((owners, share, query_columns // owners), F32),
            pltpu.VMEM((2, owners, share, 2 * key_columns // owners), F32),
            pltpu.VMEM((key_heads, group * share, head_dim), F32),
            pltpu.VMEM((key_heads, group * share, head_dim), F32),
            pltpu.VMEM((rows_dev * key_heads, positions, head_dim), BF16),
            pltpu.VMEM((rows_dev * key_heads, positions, head_dim), BF16),
            fetch_sems,
        ],
        moved=10e6,
    )(length, trig, kept, arrived, *all_factors, near, *far, far_late, block_3, w_out)

    heads_x = swapped(heads, "dp", 2)
    heads_core = swapped(heads, "dp", 1)
    last_2, block_1 = fetched(heads, (2, 6, 2), (1, 0, 4))
    heads_x, _ = lax.optimization_barrier((heads_x, block_1))
    heads_both = swapped(heads_x, "dp", 1)
    message = shape((both, part + rank), BF16)
    summed = shape((both, part + rank), F32)
    send_3, low, all_rows, last_1 = kernel_call(
        functools.partial(far_output_body, 1, 4 * eighth),
        (
            message,
            shape((both, rank), F32),
            shape((both, w_out.shape[0]), BF16),
            weight_block(4),
        ),
        [vmem_spec()] * 9 + [any_spec(), hbm_spec()],
        [pltpu.VMEM((both, w_out.shape[0]), F32), fetch_sems],
        mib=8,
        moved=10e6,
    )(heads, heads_core, heads_x, heads_both, *all_factors, block_3, block_1, w_out)
    far_3 = swapped(send_3, "tensor", 3)

    def next_output(*weights):
        return kernel_call(
            next_output_body,
            (message,),
            [vmem_spec()] * (2 + len(weights)),
            mib=8,
            moved=40e6,
        )(all_rows, low, *weights)[0]

    def added(total, far_part, moved):
        return kernel_call(add_far_body, (summed,), [vmem_spec()] * 2, mib=8, moved=moved)(
            total, far_part
        )[0]

    far_2 = swapped(next_output(block_2, last_2), "tensor", 2)
    far_1 = swapped(next_output(block_1, last_1), "tensor", 1)
    (total,) = kernel_call(
        own_output_body,
        (summed,),
        [vmem_spec()] * 3 + [hbm_spec()],
        [weight_block(6), pltpu.SemaphoreType.DMA((6,))],
        mib=12,
        moved=40e6,
    )(all_rows, low, own_first, w_out)
    total = added(added(total, far_3, 40e6), far_2, 40e6)
    (done,) = kernel_call(
        functools.partial(finish_body, rows_dev),
        (shape((both, part), BF16),),
        [vmem_spec()] * 3,
        mib=8,
    )(total, far_1, b_out)
    parts = [done] + [swapped(done, "tensor", mask) for mask in (1, 2, 3)]
    return kernel_call(
        place_body,
        (shape((rows, out_columns), BF16), shape((rows, out_columns), BF16)),
        [vmem_spec()] * 4,
        [pltpu.SemaphoreType.DMA((4, 2))],
        out_specs=(hbm_spec(), hbm_spec()),
    )(*parts)


def takes_joined(mesh):
    return mesh.shape["dp"] == 4 and mesh.shape["tensor"] == 4


def solution(mesh):
    in_specs = (
        P("groups", "dp"),
        P("groups", "dp"),
        P("dp"),
        P("dp", "tensor"),
        P("dp", "tensor"),
        P("dp", "tensor"),
        P("tensor", "dp"),
        P(("dp", "tensor"), None),
        P(None, ("tensor", "dp")),
        P(("dp", "tensor"), None),
        P(None, ("tensor", "dp")),
        P(("dp", "tensor"), None),
        P(None, ("tensor", "dp")),
        P(("tensor", "dp"), None),
        P(None, ("dp", "tensor")),
        P(("groups", "dp"), None, "tensor", None),
        P(("groups", "dp"), None, "tensor", None),
        P(("groups", "dp")),
    )
    out_specs = (P("groups", "dp"), P("groups", "dp"))
    return jax.shard_map(
        on_device_joined if takes_joined(mesh) else on_device,
        mesh=mesh,
        in_specs=in_specs,
        out_specs=out_specs,
        check_vma=False,
    )
```

```python
import functools
import math

import jax
import jax.numpy as jnp
import numpy as np
from jax import lax
from jax.experimental import pallas as pl
from jax.experimental.pallas import tpu as pltpu
from jax.sharding import PartitionSpec as P

D = 16384


ADAPTER_SCALE = 2.0
ROPE_BASE = 500000.0
EPS = 1e-05
MASKED_FILLER = -1e30
BF16 = jnp.bfloat16
F32 = jnp.float32


def joined_2(part, axis, combine):
    gathered = jax.tree.map(lambda a: lax.all_gather(a, axis), part)

    def take(source):
        return jax.tree.map(lambda a: lax.dynamic_index_in_dim(a, source, 0, False), gathered)

    return lax.fori_loop(
        1, lax.axis_size(axis), lambda source, state: combine(state, take(source)), take(0)
    )


def merge_weight(frozen_weight, factor_in, factor_out):
    adapter_update = jnp.dot(factor_in, factor_out, preferred_element_type=jnp.float32)
    return (frozen_weight.astype(jnp.float32) + ADAPTER_SCALE * adapter_update).astype(jnp.bfloat16)


def rotary(vectors, positions_now):
    half_dim = vectors.shape[-1] // 2
    frequency = ROPE_BASE ** (-jnp.arange(half_dim, dtype=jnp.float32) / half_dim)
    angles = positions_now.astype(jnp.float32)[:, None] * frequency[None, :]
    cosine = jnp.cos(angles)[:, None, :]
    sine_part = jnp.sin(angles)[:, None, :]
    lower = vectors[..., :half_dim]
    upper = vectors[..., half_dim:]
    return jnp.concatenate(
        [lower * cosine - upper * sine_part, upper * cosine + lower * sine_part], axis=-1
    )


def combine_partial(earlier, later):
    highest = jnp.maximum(earlier[0], later[0])
    weight_a = jnp.exp(earlier[0] - highest)
    weight_b = jnp.exp(later[0] - highest)
    return (
        highest,
        earlier[1] * weight_a + later[1] * weight_b,
        earlier[2] * weight_a[..., None] + later[2] * weight_b[..., None],
    )


def on_device(
    hidden_first,
    hidden_second,
    norm_gain,
    query_weight,
    w_key,
    w_value,
    w_out,
    a_query,
    b_query,
    a_key,
    b_key,
    a_value,
    b_value,
    a_out,
    b_out,
    cache_keys,
    cache_values,
    lengths,
):
    tensor_parts = (
        lax.all_gather(a_query, "tensor", axis=0, tiled=True),
        lax.all_gather(a_key, "tensor", axis=0, tiled=True),
        lax.all_gather(a_value, "tensor", axis=0, tiled=True),
        lax.all_gather(b_out, "tensor", axis=1, tiled=True),
    )
    data_parts = (
        lax.all_gather(b_query, "dp", axis=1, tiled=True),
        lax.all_gather(b_key, "dp", axis=1, tiled=True),
        lax.all_gather(b_value, "dp", axis=1, tiled=True),
        lax.all_gather(a_out, "dp", axis=0, tiled=True),
    )
    merged_qkv = jnp.concatenate(
        [
            merge_weight(query_weight, tensor_parts[0], data_parts[0]),
            merge_weight(w_key, tensor_parts[1], data_parts[1]),
            merge_weight(w_value, tensor_parts[2], data_parts[2]),
        ],
        axis=1,
    )
    merged_output = merge_weight(w_out, data_parts[3], tensor_parts[3])
    n_tensor = lax.axis_size("tensor")
    tensor_index = lax.axis_index("tensor")
    rows_dev, key_value_heads, cache_span, head_dim = cache_keys.shape
    query_cols = query_weight.shape[1]
    key_cols = w_key.shape[1]
    joint_cols = query_cols + 2 * key_cols
    heads_here = query_cols // head_dim
    all_heads = heads_here * n_tensor
    group_size = all_heads // key_value_heads
    score_scale = 1.0 / math.sqrt(head_dim)
    cache_positions = tensor_index * cache_span + jnp.arange(cache_span, dtype=jnp.int32)
    cache_valid = cache_positions[None, :] < lengths[:, None]
    first_owner = tensor_index == 0
    fresh_keys = []
    fresh_values = []
    results = []
    for step_index, hidden in enumerate((hidden_first, hidden_second)):
        values_f = hidden.astype(jnp.float32)
        squares = lax.psum(jnp.sum(values_f * values_f, axis=1), "dp")
        normed = (
            values_f * lax.rsqrt(squares / D + EPS)[:, None] * norm_gain.astype(jnp.float32)
        ).astype(jnp.bfloat16)
        projected = lax.psum_scatter(
            jnp.dot(normed, merged_qkv, preferred_element_type=jnp.float32),
            "dp",
            scatter_dimension=0,
            tiled=True,
        ).astype(jnp.bfloat16)
        joined = lax.all_gather(projected, "tensor", axis=1, tiled=True).reshape(
            rows_dev, n_tensor, joint_cols
        )
        queries = joined[:, :, :query_cols].reshape(rows_dev, all_heads, head_dim)
        key_now = joined[:, :, query_cols : query_cols + key_cols].reshape(
            rows_dev, key_value_heads, head_dim
        )
        value_now = joined[:, :, query_cols + key_cols :].reshape(
            rows_dev, key_value_heads, head_dim
        )
        positions_now = lengths + step_index
        queries = rotary(queries.astype(jnp.float32), positions_now).astype(jnp.bfloat16)
        queries = queries.reshape(rows_dev, key_value_heads, group_size, head_dim)
        fresh_keys.append(rotary(key_now.astype(jnp.float32), positions_now).astype(jnp.bfloat16))
        fresh_values.append(value_now)
        cache_scores = (
            jnp.einsum("rkgd,rksd->rkgs", queries, cache_keys, preferred_element_type=jnp.float32)
            * score_scale
        )
        cache_scores = jnp.where(cache_valid[:, None, None, :], cache_scores, MASKED_FILLER)
        new_scores = (
            jnp.einsum(
                "rkgd,rknd->rkgn",
                queries,
                jnp.stack(fresh_keys, axis=2),
                preferred_element_type=jnp.float32,
            )
            * score_scale
        )
        new_scores = jnp.where(first_owner, new_scores, MASKED_FILLER)
        highest = jnp.maximum(jnp.max(cache_scores, axis=-1), jnp.max(new_scores, axis=-1))
        cache_weights = jnp.where(
            cache_valid[:, None, None, :], jnp.exp(cache_scores - highest[..., None]), 0.0
        )
        new_weights = jnp.where(first_owner, jnp.exp(new_scores - highest[..., None]), 0.0)
        totals = jnp.sum(cache_weights, axis=-1) + jnp.sum(new_weights, axis=-1)
        weighted = jnp.einsum(
            "rkgs,rksd->rkgd", cache_weights, cache_values, preferred_element_type=jnp.float32
        )
        weighted = weighted + jnp.einsum(
            "rkgn,rknd->rkgd",
            new_weights,
            jnp.stack(fresh_values, axis=2),
            preferred_element_type=jnp.float32,
        )
        highest = highest.reshape(rows_dev, all_heads)
        totals = totals.reshape(rows_dev, all_heads)
        weighted = weighted.reshape(rows_dev, all_heads, head_dim)
        high_all, total_all, weighted_all = joined_2(
            (highest, totals, weighted), "tensor", combine_partial
        )
        normalized = weighted_all / total_all[..., None]
        own_heads = lax.dynamic_slice_in_dim(normalized, tensor_index * heads_here, heads_here, 1)
        heads = own_heads.reshape(rows_dev, query_cols).astype(jnp.bfloat16)
        out_terms = jnp.dot(
            lax.all_gather(heads, "dp", axis=0, tiled=True),
            merged_output,
            preferred_element_type=jnp.float32,
        )
        attn_out = lax.psum(out_terms, "tensor").astype(jnp.bfloat16)
        results.append(attn_out)
    return (results[0], results[1])

def swapped(array, axis, mask):
    size = lax.axis_size(axis)
    return lax.ppermute(array, axis, [(k, k ^ mask) for k in range(size)])


def vmem_spec():
    return pl.BlockSpec(memory_space=pltpu.VMEM)


def any_spec():
    return pl.BlockSpec(memory_space=pl.ANY)


def hbm_spec():
    return pl.BlockSpec(memory_space=pltpu.HBM)


def in_hbm(*arrays):
    return [pltpu.with_memory_space_constraint(array, pltpu.HBM) for array in arrays]


def cost(moved):
    return pl.CostEstimate(flops=0, bytes_accessed=int(moved), transcendentals=0)


def kernel_call(body, outs, in_specs, scratch=(), mib=12, out_specs=None, moved=0):
    return pl.pallas_call(
        body,
        out_shape=outs,
        in_specs=in_specs,
        out_specs=out_specs or tuple(vmem_spec() for _ in outs),
        scratch_shapes=list(scratch),
        cost_estimate=cost(moved),
        compiler_params=pltpu.CompilerParams(vmem_limit_bytes=mib << 20),
    )


def aligned(start, size, unit):
    return pl.ds(pl.multiple_of(start, unit), size)


def split_sum(total, width):
    high = total.astype(BF16).astype(F32)
    rest = total - high
    middle = rest.astype(BF16).astype(F32)
    low = rest - middle
    lane = lax.broadcasted_iota(jnp.int32, (total.shape[0], width), 1)
    return jnp.where(
        lane == 0, high, jnp.where(lane == 1, middle, jnp.where(lane == 2, low, 0.0))
    )


def low_places(shape, rows, place):
    blocks, span, _ = shape
    first = blocks - -(-3 * rows // span)
    for part in range(0, rows, 16):
        flat = place * rows + part
        yield first + flat // span, flat % span, part


def prepare_body(
    rows_dev,
    first_ref,
    second_ref,
    gain_ref,
    a_query_ref,
    a_key_ref,
    a_value_ref,
    keys_ref,
    values_ref,
    b_query_ref,
    b_key_ref,
    b_value_ref,
    a_out_ref,
    _,
    scaled_ref,
    squares_ref,
    low_ref,
    near,
    far_1,
    far_2,
    far_3,
    far_late,
    factors_ref,
    hidden,
    gain_held,
    a_held,
    sems,
):
    tensor_index = lax.axis_index("tensor")
    heads_here = keys_ref.shape[1] // lax.axis_size("tensor")
    rank = a_query_ref.shape[1]
    wide = b_query_ref.shape[1]
    narrow = b_key_ref.shape[0]

    def begun(group, pairs):
        copies = [pltpu.make_async_copy(*pair, sems.at[group]) for pair in pairs]
        for copy in copies:
            copy.start()
        return copies

    inputs = begun(
        0, [(first_ref, hidden.at[0]), (second_ref, hidden.at[1]), (gain_ref, gain_held)]
    )
    inputs += begun(
        1,
        [(ref, a_held.at[place]) for place, ref in enumerate((a_query_ref, a_key_ref, a_value_ref))],
    )
    moves = []
    for mask, far in enumerate((near, far_1, far_2, far_3)):
        head = jnp.bitwise_xor(tensor_index, mask) * heads_here
        for kind, cache in enumerate((keys_ref, values_ref)):
            for row in range(rows_dev):
                late = mask == 3 and (kind == 1 or row == rows_dev - 1)
                if late:
                    start = (row if kind == 1 else rows_dev) * heads_here
                else:
                    start = (kind * rows_dev + row) * heads_here
                target = far_late if late else far
                moves.append(
                    (cache.at[row, pl.ds(head, heads_here)], target.at[pl.ds(start, heads_here)])
                )
    moves.append((b_query_ref, factors_ref.at[:, pl.ds(0, wide)]))
    for place, ref in enumerate((b_key_ref, b_value_ref)):
        moves.append((ref, factors_ref.at[pl.ds(place * narrow, narrow), pl.ds(wide, rank)]))
    for piece in range(a_out_ref.shape[0] // rank):
        moves.append(
            (
                a_out_ref.at[pl.ds(piece * rank, rank)],
                factors_ref.at[:, pl.ds(wide + (piece + 1) * rank, rank)],
            )
        )
    moves = begun(2, moves)
    @pl.when(tensor_index >= 0)
    def scaled():
        for copy in inputs[:3]:
            copy.wait()
        rows, width = first_ref.shape
        pieces = []
        sums = [jnp.zeros((rows, 128), F32), jnp.zeros((rows, 128), F32)]

        def by_owner(pair):
            ordered = []
            for owner in range(rows // rows_dev):
                for part in pair:
                    ordered.append(part[owner * rows_dev : (owner + 1) * rows_dev])
            return jnp.concatenate(ordered, axis=0)

        for piece in range(width // 128):
            columns = slice(piece * 128, (piece + 1) * 128)
            steps = [hidden[step, :, columns].astype(F32) for step in range(2)]
            sums = [total + step * step for total, step in zip(sums, steps)]
            gain = gain_held[piece : piece + 1, :].astype(F32)
            scaled_ref[:, columns] = by_owner([step * gain for step in steps]).astype(BF16)
        squares_ref[...] = by_owner(sums)
        for copy in inputs[3:]:
            copy.wait()
        depth = a_query_ref.shape[0]
        own = scaled_ref[:, aligned(tensor_index * depth, depth, 128)]
        low_rows = scaled_ref.shape[0]
        for place in range(3):
            low = jnp.dot(own, a_held[place], preferred_element_type=F32)
            low_ref[:, place * rank : (place + 1) * rank] = low
            for far in (far_1, far_2, far_3):
                for at, row, part in low_places(far.shape, low_rows, place):
                    far[at, row : row + 16, :] = low[part : part + 16].astype(BF16)

    for copy in moves:
        copy.wait()


def project_body(
    rows_dev,
    lengths_ref,
    scaled_ref,
    query_ref,
    key_ref,
    value_ref,
    sums_ref,
    trig_ref,
    length_ref,
    ring,
    lengths_held,
    ring_sem,
    held_sem,
):
    slots, depth, columns = ring.shape
    chunks = query_ref.shape[0] // depth

    def fetch(chunk):
        slot = chunk % slots
        return pltpu.make_async_copy(
            query_ref.at[pl.ds(chunk * depth, depth)], ring.at[slot], ring_sem.at[slot]
        )

    for chunk in range(min(slots, chunks)):
        fetch(chunk).start()
    lengths_copy = pltpu.make_async_copy(lengths_ref, lengths_held, held_sem.at[0])
    lengths_copy.start()
    lengths_copy.wait()
    shape = length_ref.shape
    half = shape[1] // 2
    row = lax.broadcasted_iota(jnp.int32, shape, 0)
    lane = lax.broadcasted_iota(jnp.int32, shape, 1)
    length = jnp.zeros(shape, jnp.int32)
    for place in range(rows_dev):
        length = length + jnp.where(row % rows_dev == place, lengths_held[place], 0)
    length_ref[...] = length
    exponent = (lane % half).astype(F32) / half
    frequency = jnp.exp(exponent * (-math.log(ROPE_BASE)))
    angles = (length + row // rows_dev).astype(F32) * frequency
    sine = jnp.sin(angles)
    trig_ref[: shape[0], :] = jnp.cos(angles)
    trig_ref[shape[0] :, :] = jnp.where(lane < half, -sine, sine)
    place = columns
    for held in (key_ref, value_ref):
        sums_ref[:, place : place + held.shape[1]] = jnp.dot(
            scaled_ref[...], held[...], preferred_element_type=F32
        )
        place += held.shape[1]
    for chunk in range(chunks):
        fetch(chunk).wait()
        term = jnp.dot(
            scaled_ref[:, chunk * depth : (chunk + 1) * depth],
            ring[chunk % slots],
            preferred_element_type=F32,
        )
        if chunk == 0:
            sums_ref[:, :columns] = term
        else:
            sums_ref[:, :columns] += term
        if chunk + slots < chunks:
            fetch(chunk + slots).start()


def first_send_body(sums_ref, low_ref, squares_ref, far_1, far_2, far_3, send_ref, keep_ref, full):
    core = lax.rem(lax.axis_index("dp"), 2)
    columns = sums_ref.shape[1]
    rows, low_columns = low_ref.shape
    rank = low_columns // 3
    full[:, :columns] = sums_ref[...]
    for place in range(3):
        low = low_ref[:, place * rank : (place + 1) * rank]
        for far in (far_1, far_2, far_3):
            low = low + jnp.concatenate(
                [
                    far[at, row : row + 16, :].astype(F32)
                    for at, row, _ in low_places(far.shape, rows, place)
                ],
                axis=0,
            )
        full[:, columns + place * rank : columns + (place + 1) * rank] = low
    full[:, columns + low_columns :] = split_sum(
        jnp.sum(squares_ref[...], axis=1, keepdims=True), 128
    )
    share = rows // 4
    other = 1 - core
    send_ref[...] = jnp.concatenate(
        [
            full[aligned(other * share, share, 8), :],
            full[aligned((other + 2) * share, share, 8), :],
        ],
        axis=0,
    ).astype(BF16)
    keep_ref[:share, :] = full[aligned(core * share, share, 8), :]
    keep_ref[share:, :] = full[aligned((core + 2) * share, share, 8), :]


def second_send_body(keep_ref, arrived_ref, send_ref, kept_ref, full):
    chip = lax.axis_index("dp") // 2
    full[...] = keep_ref[...] + arrived_ref[...].astype(F32)
    full[:, -128:] = split_sum(jnp.sum(full[:, -128:], axis=1, keepdims=True), 128)
    share = full.shape[0] // 2
    send_ref[...] = full[aligned((1 - chip) * share, share, 8), :].astype(BF16)
    kept_ref[...] = full[aligned(chip * share, share, 8), :]


def attend_body(
    rows_dev,
    length_ref,
    trig_ref,
    kept_ref,
    arrived_ref,
    factors_0,
    factors_1,
    factors_2,
    factors_3,
    near,
    far_1,
    far_2,
    far_3,
    far_late,
    _,
    weight_ref,
    heads_ref,
    block_ref,
    low_query,
    low_narrow,
    turned,
    mixed,
    keys_all,
    values_all,
    sems,
):
    dp_index = lax.axis_index("dp")
    tensor_index = lax.axis_index("tensor")
    copies = fetch_copies(weight_ref, jnp.bitwise_xor(tensor_index, 2), 0, block_ref, sems)
    for copy in copies:
        copy.start()
    @pl.when(dp_index >= 0)
    def attended():
        rows = 2 * rows_dev
        span, head_dim = near.shape[1:]
        key_heads = keys_all.shape[0] // rows_dev
        query_columns = heads_ref.shape[1]
        heads = query_columns // head_dim
        group = heads // key_heads
        sources = lax.axis_size("tensor")
        rank = factors_0.shape[0]
        owners = lax.axis_size("dp")
        wide = query_columns // owners
        narrow = key_heads * head_dim // owners

        for place in range(rows_dev * key_heads):
            last = place - (rows_dev - 1) * key_heads
            for mask, block in enumerate((near, far_1, far_2, far_3)):
                rows_here = slice(mask * span, (mask + 1) * span)
                key_block, value_block = block, block
                key_place, value_place = place, rows_dev * key_heads + place
                if mask == 3:
                    value_block, value_place = far_late, place
                    if last >= 0:
                        key_block, key_place = far_late, rows_dev * key_heads + last
                keys_all[place, rows_here, :] = key_block[key_place]
                values_all[place, rows_here, :] = value_block[value_place]

        total = kept_ref[...] + arrived_ref[...].astype(F32)
        joint = query_columns + 2 * key_heads * head_dim
        squares = jnp.sum(total[:, -128:], axis=1, keepdims=True)
        scale = lax.rsqrt(squares / D + EPS)
        lows = [
            total[:, joint + place * rank : joint + (place + 1) * rank].astype(BF16)
            for place in range(3)
        ]
        for mask, factors in enumerate((factors_0, factors_1, factors_2, factors_3)):
            owner = jnp.bitwise_xor(dp_index, mask)
            low_query[owner] = jnp.dot(lows[0], factors[:, :wide], preferred_element_type=F32)
            pair = factors[:, wide : wide + 2 * narrow]
            for place in range(2):
                low_narrow[place, owner] = lax.dot_general(
                    lows[place + 1], pair, (((1,), (1,)), ((), ())), preferred_element_type=F32
                )
        cosine = trig_ref[:rows, :]
        sine = trig_ref[rows:, :]

        def turn(vector):
            return vector * cosine + pltpu.roll(vector, head_dim // 2, 1) * sine

        def rounded(vector):
            return vector.astype(BF16).astype(F32)

        for head in range(heads):
            column = head * head_dim
            owner, inner = column // wide, column % wide
            vector = (
                total[:, column : column + head_dim]
                + ADAPTER_SCALE * low_query[owner, :, inner : inner + head_dim]
            )
            start = (head % group) * rows
            turned[head // group, start : start + rows, :] = turn(rounded(vector * scale))

        lane = lax.broadcasted_iota(jnp.int32, (rows, head_dim), 1)
        per_head = head_dim // narrow
        fresh = [[], []]
        for place in range(2):
            for head in range(key_heads):
                low = jnp.zeros((rows, head_dim), F32)
                for part in range(per_head):
                    piece = low_narrow[place, head * per_head + part]
                    shift = (part * narrow - place * narrow) % (2 * narrow)
                    if shift:
                        piece = pltpu.roll(piece, shift, 1)
                    low = jnp.where(lane // narrow == part, piece, low)
                column = query_columns + place * key_heads * head_dim + head * head_dim
                vector = rounded(
                    (total[:, column : column + head_dim] + ADAPTER_SCALE * low) * scale
                )
                fresh[place].append(turn(vector) if place == 0 else vector)

        cached = sources * span
        width = keys_all.shape[1]
        column = lax.broadcasted_iota(jnp.int32, (1, width), 1)
        position = jnp.where(column == cached, -1, 1 << 30)
        for mask in range(sources):
            base = jnp.bitwise_xor(tensor_index, mask) * span
            inside = (column >= mask * span) & (column < (mask + 1) * span)
            position = jnp.where(inside, column - mask * span + base, position)
        step = lax.broadcasted_iota(jnp.int32, (2 * group, width), 0) % 2
        second = (step == 1) & (
            lax.broadcasted_iota(jnp.int32, (2 * group, width), 1) == cached + 1
        )
        score_scale = 1.0 / math.sqrt(head_dim)
        for row in range(rows_dev):
            valid = (position < length_ref[row : row + 1, :1]) | second
            for head in range(key_heads):
                place = row * key_heads + head
                for joined, parts in ((keys_all, fresh[0]), (values_all, fresh[1])):
                    joined[place, cached:, :] = jnp.concatenate(
                        [
                            parts[head][row : row + 1],
                            parts[head][rows_dev + row : rows_dev + row + 1],
                            jnp.zeros((width - cached - 2, head_dim), F32),
                        ],
                        axis=0,
                    ).astype(BF16)
                query = turned[head, pl.ds(row, 2 * group, stride=rows_dev), :].astype(BF16)
                scores = (
                    lax.dot_general(
                        query,
                        keys_all[place],
                        (((1,), (1,)), ((), ())),
                        preferred_element_type=F32,
                    )
                    * score_scale
                )
                scores = jnp.where(valid, scores, MASKED_FILLER)
                highest = jnp.max(scores, axis=1, keepdims=True)
                weights = jnp.where(valid, jnp.exp(scores - highest), 0.0)
                totals = jnp.sum(weights, axis=1, keepdims=True)
                weighted = jnp.dot(
                    weights.astype(BF16), values_all[place], preferred_element_type=F32
                )
                mixed[head, pl.ds(row, 2 * group, stride=rows_dev), :] = weighted / totals
        for head in range(heads):
            start = (head % group) * rows
            heads_ref[:, head * head_dim : (head + 1) * head_dim] = mixed[
                head // group, start : start + rows, :
            ].astype(BF16)

    for copy in copies:
        copy.wait()


def fetch_copies(weight_ref, target, first, block_ref, sems):
    depth, part = block_ref.shape
    pieces = sems.shape[0]
    rows = depth // pieces
    return [
        pltpu.make_async_copy(
            weight_ref.at[
                pl.ds(first + piece * rows, rows), aligned(target * part, part, 128)
            ],
            block_ref.at[pl.ds(piece * rows, rows)],
            sems.at[piece],
        )
        for piece in range(pieces)
    ]


def fetch_body(pieces, weight_ref, _, *blocks_and_sems):
    *blocks, sems = blocks_and_sems
    copies = []
    for place, ((mask, first), block_ref) in enumerate(zip(pieces, blocks)):
        target = jnp.bitwise_xor(lax.axis_index("tensor"), mask)
        copies += fetch_copies(weight_ref, target, first, block_ref, sems.at[place])
    for copy in copies:
        copy.start()
    for copy in copies:
        copy.wait()


def product(rows_ref, *blocks):
    width = math.gcd(blocks[0].shape[1], 512)
    results = []
    for start in range(0, blocks[0].shape[1], width):
        first, result = 0, None
        for block in blocks:
            depth = block.shape[0]
            term = jnp.dot(
                rows_ref[:, first : first + depth],
                block[:, start : start + width],
                preferred_element_type=F32,
            )
            result = term if result is None else result + term
            first += depth
        results.append(result)
    return jnp.concatenate(results, axis=1)


def far_output_body(
    mask,
    first,
    heads_0,
    heads_1,
    heads_2,
    heads_3,
    factors_0,
    factors_1,
    factors_2,
    factors_3,
    block_ref,
    _,
    weight_ref,
    send_ref,
    low_ref,
    all_rows,
    fetched_ref,
    wide_rows,
    sems,
):
    dp_index = lax.axis_index("dp")
    target = jnp.bitwise_xor(lax.axis_index("tensor"), mask)
    copies = fetch_copies(weight_ref, target, first, fetched_ref, sems)
    for copy in copies:
        copy.start()
    @pl.when(dp_index >= 0)
    def multiplied():
        share = heads_0.shape[0]
        for distance, part in enumerate((heads_0, heads_1, heads_2, heads_3)):
            owner = jnp.bitwise_xor(dp_index, distance)
            wide_rows[aligned(owner * share, share, 8), :] = part[...].astype(F32)
        all_rows[...] = wide_rows[...].astype(BF16)
        rank = factors_0.shape[0]
        block = all_rows.shape[1] // lax.axis_size("dp")
        pieces = block // rank
        base = factors_0.shape[1] - pieces * rank
        low = jnp.zeros((all_rows.shape[0], rank), F32)
        for distance, factors in enumerate((factors_0, factors_1, factors_2, factors_3)):
            owner = jnp.bitwise_xor(dp_index, distance)
            joined = jnp.concatenate(
                [
                    factors[:, base + piece * rank : base + (piece + 1) * rank]
                    for piece in range(pieces)
                ],
                axis=0,
            )
            low = low + jnp.dot(
                all_rows[:, aligned(owner * block, block, 128)],
                joined,
                preferred_element_type=F32,
            )
        low_ref[...] = low
        part = block_ref.shape[1]
        send_ref[:, :part] = product(all_rows, block_ref).astype(BF16)
        send_ref[:, part:] = low.astype(BF16)

    for copy in copies:
        copy.wait()


def next_output_body(all_rows, low_ref, *blocks_and_result):
    *blocks, result_ref = blocks_and_result
    part = blocks[0].shape[1]
    result_ref[:, :part] = product(all_rows, *blocks).astype(result_ref.dtype)
    result_ref[:, part:] = low_ref[...].astype(result_ref.dtype)


def own_output_body(all_rows, low_ref, first_ref, weight_ref, result_ref, held, sems):
    tensor_index = lax.axis_index("tensor")
    done = first_ref.shape[0]
    copies = fetch_copies(weight_ref, tensor_index, done, held, sems)
    for copy in copies:
        copy.start()
    part = held.shape[1]
    rows = held.shape[0] // len(copies)

    @pl.when(tensor_index >= 0)
    def multiplied():
        result_ref[:, part:] = low_ref[...]
        result_ref[:, :part] = product(all_rows, first_ref)

    for piece, copy in enumerate(copies):
        copy.wait()
        here = slice(piece * rows, (piece + 1) * rows)
        result_ref[:, :part] += jnp.dot(
            all_rows[:, done + piece * rows : done + (piece + 1) * rows],
            held[here, :],
            preferred_element_type=F32,
        )


def add_far_body(keep_ref, far, sum_ref):
    sum_ref[...] = keep_ref[...] + far[...].astype(F32)


def finish_body(rows_dev, sum_ref, far_1, b_out_ref, part_ref):
    total = sum_ref[...] + far_1[...].astype(F32)
    part = b_out_ref.shape[1]
    low = total[:, part:].astype(BF16)
    result = total[:, :part] + ADAPTER_SCALE * jnp.dot(
        low, b_out_ref[...], preferred_element_type=F32
    )
    pieces = []
    for step in range(2):
        for owner in range(result.shape[0] // (2 * rows_dev)):
            start = (2 * owner + step) * rows_dev
            pieces.append(result[start : start + rows_dev])
    part_ref[...] = jnp.concatenate(pieces, axis=0).astype(BF16)


def place_body(part_0, part_1, part_2, part_3, first_ref, second_ref, sems):
    tensor_index = lax.axis_index("tensor")
    rows = first_ref.shape[0]
    copies = []
    for mask, part in enumerate((part_0, part_1, part_2, part_3)):
        width = part.shape[1]
        columns = aligned(jnp.bitwise_xor(tensor_index, mask) * width, width, 128)
        for step, target in enumerate((first_ref, second_ref)):
            copies.append(
                pltpu.make_async_copy(
                    part.at[pl.ds(step * rows, rows)],
                    target.at[:, columns],
                    sems.at[mask, step],
                )
            )
    for copy in copies:
        copy.start()
    for copy in copies:
        copy.wait()


def on_device_joined(
    hidden_first,
    hidden_second,
    norm_gain,
    query_weight,
    w_key,
    w_value,
    w_out,
    a_query,
    b_query,
    a_key,
    b_key,
    a_value,
    b_value,
    a_out,
    b_out,
    cache_keys,
    cache_values,
    lengths,
):
    shape = jax.ShapeDtypeStruct
    rows, width = hidden_first.shape
    rows_dev, all_key_heads, span, head_dim = cache_keys.shape
    n_tensor = lax.axis_size("tensor")
    key_heads = all_key_heads // n_tensor
    rank = a_query.shape[1]
    query_columns = query_weight.shape[1]
    key_columns = w_key.shape[1]
    joint = query_columns + 2 * key_columns
    both = 2 * rows
    share = 2 * rows_dev
    low_columns = 3 * rank
    blocks = 2 * rows_dev * key_heads
    low_blocks = -(-3 * both // span)
    pack_columns = b_query.shape[1] + rank + a_out.shape[0]

    scaled, squares, low, near, far_1, far_2, far_3, far_late, factors = kernel_call(
        functools.partial(prepare_body, rows_dev),
        (
            shape((both, width), BF16),
            shape((both, 128), F32),
            shape((both, low_columns), F32),
            shape((blocks, span, head_dim), BF16),
            shape((blocks + low_blocks, span, head_dim), BF16),
            shape((blocks + low_blocks, span, head_dim), BF16),
            shape((blocks // 2 - key_heads + low_blocks, span, head_dim), BF16),
            shape((blocks // 2 + key_heads, span, head_dim), BF16),
            shape((rank, pack_columns), BF16),
        ),
        [hbm_spec()] * 13,
        [
            pltpu.VMEM((2, rows, width), BF16),
            pltpu.VMEM((width // 128, 128), BF16),
            pltpu.VMEM((3,) + a_query.shape, BF16),
            pltpu.SemaphoreType.DMA((3,)),
        ],
        moved=60e6,
    )(
        *in_hbm(
            hidden_first,
            hidden_second,
            norm_gain.reshape(width // 128, 128),
            a_query,
            a_key,
            a_value,
            cache_keys,
            cache_values,
            b_query,
            b_key.T,
            b_value.T,
            a_out,
            w_out,
        )
    )
    far = [swapped(part, "tensor", mask) for mask, part in ((1, far_1), (2, far_2), (3, far_3))]
    factors_x = swapped(factors, "dp", 2)
    factors_core = swapped(factors, "dp", 1)

    depth = math.gcd(width, 256)
    sums, trig, length = kernel_call(
        functools.partial(project_body, rows_dev),
        (
            shape((both, joint), F32),
            shape((2 * share, head_dim), F32),
            shape((share, head_dim), jnp.int32),
        ),
        [hbm_spec(), vmem_spec(), hbm_spec(), vmem_spec(), vmem_spec()],
        [
            pltpu.VMEM((4, depth, query_columns), BF16),
            pltpu.SMEM((rows_dev,), jnp.int32),
            pltpu.SemaphoreType.DMA((4,)),
            pltpu.SemaphoreType.DMA((1,)),
        ],
        moved=2 * width * joint,
        mib=16,
    )(*in_hbm(lengths), scaled, *in_hbm(query_weight), w_key, w_value)
    heads_here = query_columns // head_dim
    out_columns = w_out.shape[1]
    part = out_columns // n_tensor
    eighth = w_out.shape[0] // 8

    def weight_block(eighths):
        return pltpu.VMEM((eighths * eighth, part), BF16)

    (w_out,) = in_hbm(w_out)
    fetch_sems = pltpu.SemaphoreType.DMA((4,))

    def fetched(after, *pieces):
        return kernel_call(
            functools.partial(
                fetch_body, [(mask, first * eighth) for mask, first, _ in pieces]
            ),
            tuple(weight_block(eighths) for _, _, eighths in pieces),
            [hbm_spec(), any_spec()],
            [pltpu.SemaphoreType.DMA((len(pieces), 4))],
            mib=4,
            moved=2 * sum(eighths for _, _, eighths in pieces) * eighth * part,
        )(w_out, after)

    extended = joint + low_columns + 128
    send, keep = kernel_call(
        first_send_body,
        (shape((rows, extended), BF16), shape((rows, extended), F32)),
        [vmem_spec()] * 6,
        [pltpu.VMEM((both, extended), F32)],
    )(sums, low, squares, *far)
    factors_x, far_late, send = lax.optimization_barrier((factors_x, far_late, send))
    far_late = swapped(far_late, "tensor", 3)
    factors_both = swapped(factors_x, "dp", 1)
    all_factors = (factors, factors_core, factors_x, factors_both)
    arrived = swapped(send, "dp", 1)
    send, kept = kernel_call(
        second_send_body,
        (shape((share, extended), BF16), shape((share, extended), F32)),
        [vmem_spec()] * 2,
        [pltpu.VMEM((rows, extended), F32)],
    )(keep, arrived)
    arrived = swapped(send, "dp", 2)
    block_3, own_first = fetched(send, (3, 0, 8), (0, 0, 2))
    group = heads_here // key_heads
    positions = n_tensor * span + 16
    owners = lax.axis_size("dp")
    heads, block_2 = kernel_call(
        functools.partial(attend_body, rows_dev),
        (shape((share, query_columns), BF16), weight_block(6)),
        [vmem_spec()] * 13 + [any_spec(), hbm_spec()],
        [
            pltpu.VMEM((owners, share, query_columns // owners), F32),
            pltpu.VMEM((2, owners, share, 2 * key_columns // owners), F32),
            pltpu.VMEM((key_heads, group * share, head_dim), F32),
            pltpu.VMEM((key_heads, group * share, head_dim), F32),
            pltpu.VMEM((rows_dev * key_heads, positions, head_dim), BF16),
            pltpu.VMEM((rows_dev * key_heads, positions, head_dim), BF16),
            fetch_sems,
        ],
        moved=10e6,
    )(length, trig, kept, arrived, *all_factors, near, *far, far_late, block_3, w_out)

    heads_x = swapped(heads, "dp", 2)
    heads_core = swapped(heads, "dp", 1)
    last_2, block_1 = fetched(heads, (2, 6, 2), (1, 0, 4))
    heads_x, _ = lax.optimization_barrier((heads_x, block_1))
    heads_both = swapped(heads_x, "dp", 1)
    message = shape((both, part + rank), BF16)
    summed = shape((both, part + rank), F32)
    send_3, low, all_rows, last_1 = kernel_call(
        functools.partial(far_output_body, 1, 4 * eighth),
        (
            message,
            shape((both, rank), F32),
            shape((both, w_out.shape[0]), BF16),
            weight_block(4),
        ),
        [vmem_spec()] * 9 + [any_spec(), hbm_spec()],
        [pltpu.VMEM((both, w_out.shape[0]), F32), fetch_sems],
        mib=8,
        moved=10e6,
    )(heads, heads_core, heads_x, heads_both, *all_factors, block_3, block_1, w_out)
    far_3 = swapped(send_3, "tensor", 3)

    def next_output(*weights):
        return kernel_call(
            next_output_body,
            (message,),
            [vmem_spec()] * (2 + len(weights)),
            mib=8,
            moved=40e6,
        )(all_rows, low, *weights)[0]

    def added(total, far_part, moved):
        return kernel_call(add_far_body, (summed,), [vmem_spec()] * 2, mib=8, moved=moved)(
            total, far_part
        )[0]

    far_2 = swapped(next_output(block_2, last_2), "tensor", 2)
    far_1 = swapped(next_output(block_1, last_1), "tensor", 1)
    (total,) = kernel_call(
        own_output_body,
        (summed,),
        [vmem_spec()] * 3 + [hbm_spec()],
        [weight_block(6), pltpu.SemaphoreType.DMA((6,))],
        mib=12,
        moved=40e6,
    )(all_rows, low, own_first, w_out)
    total = added(added(total, far_3, 40e6), far_2, 40e6)
    (done,) = kernel_call(
        functools.partial(finish_body, rows_dev),
        (shape((both, part), BF16),),
        [vmem_spec()] * 3,
        mib=8,
    )(total, far_1, b_out)
    parts = [done] + [swapped(done, "tensor", mask) for mask in (1, 2, 3)]
    return kernel_call(
        place_body,
        (shape((rows, out_columns), BF16), shape((rows, out_columns), BF16)),
        [vmem_spec()] * 4,
        [pltpu.SemaphoreType.DMA((4, 2))],
        out_specs=(hbm_spec(), hbm_spec()),
    )(*parts)


def takes_joined(mesh):
    return mesh.shape["dp"] == 4 and mesh.shape["tensor"] == 4


def solution(mesh):
    in_specs = (
        P("groups", "dp"),
        P("groups", "dp"),
        P("dp"),
        P("dp", "tensor"),
        P("dp", "tensor"),
        P("dp", "tensor"),
        P("tensor", "dp"),
        P(("dp", "tensor"), None),
        P(None, ("tensor", "dp")),
        P(("dp", "tensor"), None),
        P(None, ("tensor", "dp")),
        P(("dp", "tensor"), None),
        P(None, ("tensor", "dp")),
        P(("tensor", "dp"), None),
        P(None, ("dp", "tensor")),
        P(("groups", "dp"), None, "tensor", None),
        P(("groups", "dp"), None, "tensor", None),
        P(("groups", "dp")),
    )
    out_specs = (P("groups", "dp"), P("groups", "dp"))
    return jax.shard_map(
        on_device_joined if takes_joined(mesh) else on_device,
        mesh=mesh,
        in_specs=in_specs,
        out_specs=out_specs,
        check_vma=False,
    )
```
